32 devices in a mesh: sx: 4 (over x, core), sy: 4 (over z), ch: 2 (over y).
Axes of the slice: x: 2, y: 2, z: 4, core: 2. Of those that a mesh axis runs over, the one named last changes fastest.
Arguments:
- volume: bfloat16 [512, 32, 512], P('ch', 'sx', 'sy'), may hold values from -6 to 6
- weight: bfloat16 [3, 3, 3, 512, 512], P(None, None, None, 'ch'), may hold values from -0.0546875 to 0.0546875
- bias: float32 [512], P('ch'), may hold values from -3 to 3
Outputs:
- convolved: bfloat16 [512, 32, 512], P('ch', 'sx', 'sy')
The draws below stay inside these ranges and needn't reach their ends.
All inputs are finite; a program needn't handle non-finite values.
Results may differ from the reference program's by a relative error of at most 0.001.
Values may be sent and summed in bfloat16 or wider, within the bound.
No kernel may reach another device: no remote copies, remote signals or barrier semaphores. Data moves between devices by JAX's collectives and lax.ppermute only.
A program may use at most 192 MiB of HBM per device.

```python
import jax
import jax.numpy as jnp
from jax import lax

C_IN = 512
C_OUT = 512
CZ = 16
NX = 32
NY = 32


def level_of(stream_key, shape, split, low, top_value):
    factor_of, own = 1.0, jax.random.fold_in(stream_key, 6)
    for axis_at, shards_of in split:
        heights = jnp.exp(jax.random.uniform(jax.random.fold_in(own, axis_at), (shards_of,), jnp.float32, low / len(split), top_value / len(split)))
        factor_of = factor_of * jnp.repeat(heights, shape[axis_at] // shards_of).reshape([-1 if axis == axis_at else 1 for axis in range(len(shape))])
    return factor_of


def bell_draw(rng, shape, spread, bound, split=(), held_as=jnp.bfloat16):
    values = jax.random.normal(rng, shape, jnp.float32) * spread
    if len(split) > 0:
        values = level_of(rng, shape, split, -0.22, 0.18) * values
    return jnp.clip(values, min=-bound, max=bound).astype(held_as)


def setup_inputs(seed: int = 0) -> dict:
    seeds = jax.random.split(jax.random.key(seed), 4)
    volume = bell_draw(seeds[0], (C_IN, NX, NY * CZ), 1.0, 6.0, ((0, 2), (1, 4), (2, 4)))
    weight = bell_draw(seeds[1], (3, 3, 3, C_OUT, C_IN), (27 * C_IN) ** -0.5, 0.0546875, ((3, 2),))
    bias = bell_draw(seeds[2], (C_OUT,), 0.5, 3.0, ((0, 2),), jnp.float32)
    return dict(volume=volume, weight=weight, bias=bias)


def reference(volume, weight, bias):
    cells = volume.reshape(C_IN, NX, NY, CZ).astype(jnp.float32)
    cells = jnp.transpose(cells, (1, 2, 3, 0))[None]
    filters = jnp.transpose(weight.astype(jnp.float32), (0, 1, 2, 4, 3))
    summed = lax.conv_general_dilated(
        cells,
        filters,
        (1, 1, 1),
        "SAME",
        dimension_numbers=("NDHWC", "DHWIO", "NDHWC"),
        precision=lax.Precision.HIGHEST,
        preferred_element_type=jnp.float32,
    )[0]
    summed = summed + bias.astype(jnp.float32)
    result = jnp.transpose(summed, (3, 0, 1, 2)).reshape(C_OUT, NX, NY * CZ)
    return result.astype(jnp.bfloat16)
```

```python
import functools

import jax
import jax.numpy as jnp
from jax import lax
from jax.experimental import pallas as pl
from jax.experimental.pallas import tpu as pltpu
from jax.sharding import PartitionSpec as P

CZ = 16
LANES = 128
VMEM = pl.BlockSpec(memory_space=pltpu.VMEM)
bf16, f32 = jnp.bfloat16, jnp.float32


def call(kernel, outs, args, scratch=(), flops=0, limit=24):
    outs = [jax.ShapeDtypeStruct(s, d) for s, d in outs]
    moved = sum(a.size * a.dtype.itemsize for a in [*outs, *args])
    return pl.pallas_call(
        kernel,
        out_shape=outs,
        in_specs=[VMEM] * len(args),
        out_specs=[VMEM] * len(outs),
        scratch_shapes=list(scratch),
        compiler_params=pltpu.CompilerParams(vmem_limit_bytes=limit * 2**20),
        cost_estimate=pl.CostEstimate(flops=flops, bytes_accessed=moved, transcendentals=0),
    )(*args)


def pairs(count, phase):
    found = []
    for low in range(phase, count - 1, 2):
        found += [(low, low + 1), (low + 1, low)]
    return found


def odd(axis):
    return lax.rem(lax.axis_index(axis), 2) == 1


def to_rows(v_ref, rows_ref, first_ref, second_ref, wide):
    cells_x = v_ref.shape[1]
    wide[...] = v_ref[...].astype(f32)
    for x in range(cells_x):
        rows_ref[x] = wide[:, x, :].astype(bf16)
    last = cells_x - 1

    @pl.when(odd("sx"))
    def _():
        first_ref[...] = rows_ref[0]
        second_ref[...] = rows_ref[last]

    @pl.when(jnp.logical_not(odd("sx")))
    def _():
        first_ref[...] = rows_ref[last]
        second_ref[...] = rows_ref[0]


def extended(rows, first, second):
    is_odd = odd("sx")
    before = jnp.where(is_odd, first, second)
    after = jnp.where(is_odd, second, first)
    return [before, *rows, after]


def pack(rows, start):
    cut = [r[:, start : start + CZ] for r in rows]
    part = rows[0].shape[0] // 4
    outer = jnp.concatenate([cut[0], cut[-1]], axis=1)
    folded = jnp.concatenate([outer[g * part : (g + 1) * part] for g in range(4)], axis=1)
    return jnp.concatenate([jnp.concatenate(cut[1:-1], axis=1), folded], axis=0)


def to_strips(rows_ref, first_ref, second_ref, left_ref, right_ref):
    cells_x = rows_ref.shape[0]
    rows = extended([rows_ref[x] for x in range(cells_x)], first_ref[...], second_ref[...])
    low = pack(rows, 0)
    high = pack(rows, LANES - CZ)
    is_odd = odd("sy")
    left_ref[...] = jnp.where(is_odd, low, high)
    right_ref[...] = jnp.where(is_odd, high, low)


def shifted(rows_ref, first_ref, second_ref, strips_ref, xs):
    cells_x, channels, lanes = rows_ref.shape
    part = channels // 4
    size = channels + part
    is_odd = odd("sy")
    one, two = strips_ref[0:size].astype(f32), strips_ref[size : 2 * size].astype(f32)
    before = jnp.where(is_odd, one, two)
    after = jnp.where(is_odd, two, one)
    lane = lax.broadcasted_iota(jnp.int32, (channels, lanes), 1)
    rows = extended([rows_ref[x] for x in range(cells_x)], first_ref[...], second_ref[...])

    def piece(strip, x, to):
        if 1 <= x <= cells_x:
            return pltpu.roll(strip[:channels], (to - (x - 1) * CZ) % lanes, axis=1)
        at = 0 if x == 0 else CZ
        folded = strip[channels:]
        return jnp.concatenate(
            [pltpu.roll(folded, (to - at - g * 2 * CZ) % lanes, axis=1) for g in range(4)], axis=0
        )

    for x in range(cells_x + 2):
        xs[1, x] = rows[x]
        row = rows[x].astype(f32)
        down = pltpu.roll(row, CZ, axis=1)
        xs[0, x] = jnp.where(lane < CZ, piece(before, x, 0), down).astype(bf16)
        up = pltpu.roll(row, lanes - CZ, axis=1)
        xs[2, x] = jnp.where(lane >= lanes - CZ, piece(after, x, lanes - CZ), up).astype(bf16)


def block_sum(weight_ref, xs, at, tile):
    outputs, channels = weight_ref.shape[3], xs.shape[2]
    total = None
    for a in range(3):
        for b in range(3):
            if weight_ref.shape[4] == channels:
                taps = weight_ref[a, b]
            else:
                start = pl.multiple_of(at * channels, channels)
                taps = weight_ref[a, b, :, :, pl.ds(start, channels)]
            window = jnp.concatenate([xs[b, x + a] for x in tile], axis=1)
            product = jnp.dot(
                taps.reshape(3 * outputs, channels), window, preferred_element_type=f32
            )
            total = product if total is None else total + product
    return total


def tiles_of(cells_x):
    inner = [(x, x + 1) for x in range(1, cells_x - 1, 2)]
    return [*inner, (0, cells_x - 1)]


def own_kernel(rows_ref, first_ref, second_ref, strips_ref, weight_ref, acc_ref, xs):
    at = lax.axis_index("ch")
    shifted(rows_ref, first_ref, second_ref, strips_ref, xs)
    for tile in tiles_of(rows_ref.shape[0]):
        total = block_sum(weight_ref, xs, at, tile)
        for j, x in enumerate(tile):
            acc_ref[x] = total[:, j * LANES : (j + 1) * LANES]


def other_kernel(step, final, *refs):
    rows_ref, first_ref, second_ref, strips_ref, weight_ref, acc_ref = refs[:6]
    count = lax.axis_size("ch")
    at = lax.rem(lax.axis_index("ch") + count - step, count)
    xs = refs[-2]
    shifted(rows_ref, first_ref, second_ref, strips_ref, xs)
    if final:
        bias_ref, out_ref, wide = refs[6], refs[7], refs[-1]
        outputs = bias_ref.shape[0]
        cell = lax.rem(lax.broadcasted_iota(jnp.int32, (outputs, LANES), 1), CZ)
    else:
        sum_ref = refs[6]
    for tile in tiles_of(rows_ref.shape[0]):
        total = block_sum(weight_ref, xs, at, tile)
        for j, x in enumerate(tile):
            row = acc_ref[x] + total[:, j * LANES : (j + 1) * LANES]
            if not final:
                sum_ref[x] = row
                continue
            under, mid, over = (row[c * outputs : (c + 1) * outputs] for c in range(3))
            under = jnp.where(cell == 0, 0.0, pltpu.roll(under, 1, axis=1))
            over = jnp.where(cell == CZ - 1, 0.0, pltpu.roll(over, LANES - 1, axis=1))
            wide[:, x, :] = (under + over) + mid + bias_ref[...]
    if final:
        out_ref[...] = wide[...].astype(bf16)


def per_device(volume, weight, bias):
    channels, cells_x, lanes = volume.shape
    outputs = weight.shape[3]
    count, count_x, count_y = (lax.axis_size(a) for a in ("ch", "sx", "sy"))
    strip = channels + channels // 4
    face, taps = (channels, lanes), (3 * outputs, lanes)
    flops = 2 * 27 * channels * outputs * cells_x * lanes

    def along(step):
        return [(i, (i + step) % count) for i in range(count)]

    def rows_of(block):
        return call(
            to_rows,
            [((cells_x, *face), bf16), (face, bf16), (face, bf16)],
            [block],
            [pltpu.VMEM((channels, cells_x, lanes), f32)],
        )

    others = [lax.ppermute(volume, "ch", along(step)) for step in range(1, count)]
    spread = jnp.broadcast_to(bias[:, None], (outputs, lanes))
    rows, one, two = rows_of(volume)
    first = lax.ppermute(one, "sx", pairs(count_x, 0))
    second = lax.ppermute(two, "sx", pairs(count_x, 1))
    left, right = call(to_strips, [((strip, lanes), bf16)] * 2, [rows, first, second])
    strips = jnp.concatenate(
        [lax.ppermute(left, "sy", pairs(count_y, 0)), lax.ppermute(right, "sy", pairs(count_y, 1))]
    )
    other_strips = [lax.ppermute(strips, "ch", along(step)) for step in range(1, count)]
    other_seconds = [
        lax.ppermute(
            second,
            ("sx", "ch"),
            [(x * count + i, x * count + j) for x in range(1, count_x - 1) for i, j in along(step)],
        )
        for step in range(1, count)
    ]
    def weight_of(step):
        if channels % LANES == 0:
            return weight
        at = lax.rem(lax.axis_index("ch") + count - step, count)
        return lax.dynamic_slice_in_dim(weight, at * channels, channels, axis=4)

    xs = pltpu.VMEM((3, cells_x + 2, *face), bf16)
    (acc,) = call(
        own_kernel,
        [((cells_x, *taps), f32)],
        [rows, first, second, strips, weight_of(0)],
        [xs],
        flops,
    )
    for step in range(1, count):
        block, block_one, _ = rows_of(others[step - 1])
        block_first = lax.ppermute(block_one, "sx", pairs(count_x, 0))
        args = [block, block_first, other_seconds[step - 1], other_strips[step - 1]]
        args += [weight_of(step), acc]
        final = step == count - 1
        if final:
            args.append(spread)
        (acc,) = call(
            functools.partial(other_kernel, step, final),
            [((outputs, cells_x, lanes), bf16) if final else ((cells_x, *taps), f32)],
            args,
            [xs, pltpu.VMEM((outputs, cells_x, lanes), f32)],
            flops,
        )
    return acc


def solution(mesh):
    return jax.shard_map(
        per_device,
        mesh=mesh,
        in_specs=(P("ch", "sx", "sy"), P(None, None, None, "ch", None), P("ch")),
        out_specs=P("ch", "sx", "sy"),
        check_vma=False,
    )
```

```python
import functools

import jax
import jax.numpy as jnp
from jax import lax
from jax.experimental import pallas as pl
from jax.experimental.pallas import tpu as pltpu
from jax.sharding import PartitionSpec as P

CZ = 16
LANES = 128
VMEM = pl.BlockSpec(memory_space=pltpu.VMEM)
HBM = pl.BlockSpec(memory_space=pltpu.HBM)
ANY = pl.BlockSpec(memory_space=pl.ANY)
bf16, f32 = jnp.bfloat16, jnp.float32


def call(kernel, outs, args, scratch=(), left={}, limit=24):
    return pl.pallas_call(
        kernel,
        out_shape=[jax.ShapeDtypeStruct(s, d) for s, d in outs],
        in_specs=[left.get(i, VMEM) for i in range(len(args))],
        out_specs=[VMEM] * len(outs),
        scratch_shapes=list(scratch),
        compiler_params=pltpu.CompilerParams(vmem_limit_bytes=limit * 2**20),
        cost_estimate=pl.CostEstimate(flops=0, bytes_accessed=0, transcendentals=0),
    )(*args)


def swap_near(count):
    return [i ^ 1 for i in range(count)]


def swap_far(count):
    return [None, *[i + 1 if i % 2 else i - 1 for i in range(1, count - 1)], None]


def exchange(block, axis, other, far):
    count, width = lax.axis_size(axis), lax.axis_size(other)
    partner = swap_far(count) if far else swap_near(count)
    aside = swap_near(width)
    moves = []
    for i in range(count):
        for j in range(width):
            to = (i, aside[j]) if partner[i] is None else (partner[i], j)
            if axis == "sx":
                moves.append((i * width + j, to[0] * width + to[1]))
            else:
                moves.append((j * count + i, to[1] * count + to[0]))
    return lax.ppermute(block, ("sx", "sy"), moves)


def pass_on(block, step):
    count_x, count_y, count = (lax.axis_size(a) for a in ("sx", "sy", "ch"))
    moves = []
    for x in range(count_x):
        for y in range(count_y):
            for c in range(count):
                to = (y ^ 1, c) if x in (0, count_x - 1) else (y, (c + step) % count)
                moves.append(((x * count_y + y) * count + c, (x * count_y + to[0]) * count + to[1]))
    return lax.ppermute(block, ("sx", "sy", "ch"), moves)


def odd(axis):
    return lax.rem(lax.axis_index(axis), 2) == 1


def at_end(axis):
    at = lax.axis_index(axis)
    return jnp.logical_or(at == 0, at == lax.axis_size(axis) - 1)


def to_rows(v_ref, rows_ref, near_ref, *far_ref):
    rows = jnp.swapaxes(v_ref[...], 0, 1)
    rows_ref[...] = rows
    is_odd = odd("sx")
    near_ref[...] = jnp.where(is_odd, rows[0], rows[-1])
    if far_ref:
        far_ref[0][...] = jnp.where(is_odd, rows[-1], rows[0])


def around(axis, near, far):
    is_odd = odd(axis)
    far = jnp.where(at_end(axis), jnp.zeros_like(far), far)
    return jnp.where(is_odd, near, far), jnp.where(is_odd, far, near)


def extended(rows_ref, near_ref, far_ref):
    before, after = around("sx", near_ref[...], far_ref[...])
    return [before, *[rows_ref[x] for x in range(rows_ref.shape[0])], after]


def pack(rows, start):
    cut = [r[:, start : start + CZ] for r in rows]
    part = rows[0].shape[0] // 4
    outer = jnp.concatenate([cut[0], cut[-1]], axis=1)
    folded = jnp.concatenate([outer[g * part : (g + 1) * part] for g in range(4)], axis=1)
    return jnp.concatenate([jnp.concatenate(cut[1:-1], axis=1), folded], axis=0)


def to_strips(rows_ref, near_ref, far_ref, _, near_strip_ref, far_strip_ref):
    rows = extended(rows_ref, near_ref, far_ref)
    low = pack(rows, 0)
    high = pack(rows, LANES - CZ)
    is_odd = odd("sy")
    near_strip_ref[...] = jnp.where(is_odd, low, high)
    far_strip_ref[...] = jnp.where(is_odd, high, low)


def shifted(rows, strips_ref, xs):
    channels, lanes = rows[0].shape
    last = len(rows) - 1
    size = strips_ref.shape[0] // 2
    near, far = strips_ref[0:size].astype(f32), strips_ref[size : 2 * size].astype(f32)
    before, after = around("sy", near, far)
    lane = lax.broadcasted_iota(jnp.int32, (channels, lanes), 1)

    def piece(strip, x, to):
        if 0 < x < last:
            return pltpu.roll(strip[:channels], (to - (x - 1) * CZ) % lanes, axis=1)
        at = 0 if x == 0 else CZ
        folded = strip[channels:]
        return jnp.concatenate(
            [pltpu.roll(folded, (to - at - g * 2 * CZ) % lanes, axis=1) for g in range(4)], axis=0
        )

    for x in range(last + 1):
        row = rows[x].astype(f32)
        down = pltpu.roll(row, CZ, axis=1)
        xs[0, x] = jnp.where(lane < CZ, piece(before, x, 0), down).astype(bf16)
        up = pltpu.roll(row, lanes - CZ, axis=1)
        xs[1, x] = jnp.where(lane >= lanes - CZ, piece(after, x, lanes - CZ), up).astype(bf16)


def block_sum(weight_ref, step, window, tile, along_y):
    outputs = weight_ref.shape[3]
    total = None
    for a in range(3):
        for b in along_y:
            rhs = jnp.concatenate([window(b, x + a) for x in tile], axis=1)
            channels = rhs.shape[0]
            if channels % LANES:
                taps = weight_ref[a, b, :, :, step * channels : (step + 1) * channels]
            else:
                count = lax.axis_size("ch")
                at = lax.rem(lax.axis_index("ch") + count - step, count)
                start = pl.multiple_of(at * channels, channels)
                taps = weight_ref[a, b, :, :, pl.ds(start, channels)]
            product = jnp.dot(
                taps.reshape(3 * outputs, channels), rhs, preferred_element_type=f32
            )
            total = product if total is None else total + product
    return [total[:, j * LANES : (j + 1) * LANES] for j in range(len(tile))]


def inner_tiles(cells_x):
    return [(x, x + 1) for x in range(1, cells_x - 1, 2)]


def first_kernel(rows_ref, weight_hbm, inner_ref, weight_ref, sems):
    copies = {}
    for b in (1, 0, 2):
        for a in range(3):
            here = pltpu.make_async_copy(weight_hbm.at[a, b], weight_ref.at[a, b], sems.at[a, b])
            here.start()
            copies[a, b] = here
    for a in range(3):
        copies[a, 1].wait()
    for tile in inner_tiles(rows_ref.shape[0]):
        parts = block_sum(weight_ref, 0, lambda b, x: rows_ref[x - 1], tile, (1,))
        for x, part in zip(tile, parts):
            inner_ref[x - 1] = part
    for b in (0, 2):
        for a in range(3):
            copies[a, b].wait()


def join_kernel(near_ref, far_ref, strips_ref):
    size = near_ref.shape[0]
    strips_ref[0:size] = near_ref[...]
    strips_ref[size : 2 * size] = far_ref[...]


def middle_kernel(others, *refs):
    rows_ref, near_ref, far_ref, strips_ref, weight_ref, inner_ref = refs[:6]
    other_rows = refs[6 : 6 + others]
    out_ref, outer_ref, xs = refs[6 + others :]
    rows = extended(rows_ref, near_ref, far_ref)
    shifted(rows, strips_ref, xs)
    last = rows_ref.shape[0] - 1

    def window(b, x):
        return rows[x] if b == 1 else xs[b // 2, x]

    for tile in inner_tiles(last + 1):
        sums = [block_sum(weight_ref, 0, window, tile, (0, 2))]
        for i, other_ref in enumerate(other_rows):
            sums.append(
                block_sum(weight_ref, i + 1, lambda b, x: other_ref[x - 1], tile, (1,))
            )
        for x, parts in zip(tile, zip(*sums)):
            out_ref[x - 1] = sum(parts, inner_ref[x - 1])
    for j, part in enumerate(block_sum(weight_ref, 0, window, (0, last), (1, 0, 2))):
        outer_ref[j] = part


def last_kernel(step, final, *refs):
    rows_ref, near_ref, far_ref, strips_ref, weight_ref, inner_ref, outer_ref = refs[:7]
    rows = extended(rows_ref, near_ref, far_ref)
    xs = refs[-1]
    shifted(rows, strips_ref, xs)
    last = rows_ref.shape[0] - 1
    if final:
        bias_ref, out_ref, done = refs[7:10]
        outputs = bias_ref.shape[0]
        cell = lax.rem(lax.broadcasted_iota(jnp.int32, (outputs, LANES), 1), CZ)

    def window(b, x):
        return rows[x] if b == 1 else xs[b // 2, x]

    for tile in [*inner_tiles(last + 1), (0, last)]:
        outer = tile == (0, last)
        parts = block_sum(weight_ref, step, window, tile, (1, 0, 2) if outer else (0, 2))
        for j, (x, row) in enumerate(zip(tile, parts)):
            row = row + (outer_ref[j] if outer else inner_ref[x - 1])
            if not final:
                if outer:
                    refs[8][j] = row
                else:
                    refs[7][x - 1] = row
                continue
            under, mid, over = (row[c * outputs : (c + 1) * outputs] for c in range(3))
            under = jnp.where(cell == 0, 0.0, pltpu.roll(under, 1, axis=1))
            over = jnp.where(cell == CZ - 1, 0.0, pltpu.roll(over, LANES - 1, axis=1))
            done[x] = ((under + over) + mid + bias_ref[...]).astype(bf16)
    if final:
        out_ref[...] = jnp.swapaxes(done[...], 0, 1)


def per_device(volume, weight, bias):
    channels, cells_x, lanes = volume.shape
    outputs = weight.shape[3]
    count = lax.axis_size("ch")
    strip = (channels + channels // 4, lanes)
    face, taps = (channels, lanes), (3 * outputs, lanes)
    sums = [((cells_x - 2, *taps), f32), ((2, *taps), f32)]
    xs = pltpu.VMEM((2, cells_x + 2, *face), bf16)

    def along(step):
        return [(i, (i + step) % count) for i in range(count)]

    def rows_of(block, edges):
        return call(to_rows, [((cells_x, *face), bf16)] + [(face, bf16)] * edges, [block])

    others = [lax.ppermute(volume, "ch", along(step)) for step in range(1, count)]
    spread = jnp.broadcast_to(bias[:, None], (outputs, lanes))
    if channels % LANES:
        at = lax.axis_index("ch")
        blocks = [lax.rem(at + count - step, count) * channels for step in range(count)]
        weight = jnp.concatenate(
            [lax.dynamic_slice_in_dim(weight, i, channels, axis=4) for i in blocks], axis=4
        )
    rows, near, far = rows_of(volume, 2)
    near = exchange(near, "sx", "sy", False)
    far = exchange(far, "sx", "sy", True)
    inner, weight = call(
        first_kernel,
        [sums[0], (weight.shape, bf16)],
        [rows, weight],
        [pltpu.SemaphoreType.DMA((3, 3))],
        left={1: HBM},
        limit=42,
    )
    one, two = call(to_strips, [(strip, bf16)] * 2, [rows, near, far, inner], left={3: ANY})
    one = exchange(one, "sy", "sx", False)
    two = exchange(two, "sy", "sx", True)
    other_far = [pass_on(far, step) for step in range(1, count)]
    (strips,) = call(join_kernel, [((2 * strip[0], lanes), bf16)], [one, two])
    other_strips = [lax.ppermute(strips, "ch", along(step)) for step in range(1, count)]
    other_rows, other_near = [], []
    for other in others:
        block, edge = rows_of(other, 1)
        other_rows.append(block)
        other_near.append(exchange(edge, "sx", "sy", False))
    acc = call(
        functools.partial(middle_kernel, count - 1),
        sums,
        [rows, near, far, strips, weight, inner, *other_rows],
        [xs],
    )
    for step in range(1, count):
        i, final = step - 1, step == count - 1
        args = [other_rows[i], other_near[i], other_far[i], other_strips[i], weight, *acc]
        acc = call(
            functools.partial(last_kernel, step, final),
            [((outputs, cells_x, lanes), bf16)] if final else sums,
            [*args, spread] if final else args,
            [pltpu.VMEM((cells_x, outputs, lanes), bf16), xs] if final else [xs],
        )
    return acc[0]


def solution(mesh):
    return jax.shard_map(
        per_device,
        mesh=mesh,
        in_specs=(P("ch", "sx", "sy"), P(None, None, None, "ch", None), P("ch")),
        out_specs=P("ch", "sx", "sy"),
        check_vma=False,
    )
```

```python
import functools

import jax
import jax.numpy as jnp
from jax import lax
from jax.experimental import pallas as pl
from jax.experimental.pallas import tpu as pltpu
from jax.sharding import PartitionSpec as P

CZ = 16
LANES = 128
VMEM = pl.BlockSpec(memory_space=pltpu.VMEM)
HBM = pl.BlockSpec(memory_space=pltpu.HBM)
ANY = pl.BlockSpec(memory_space=pl.ANY)
bf16, f32 = jnp.bfloat16, jnp.float32


def call(kernel, outs, args, scratch=(), left={}, limit=24, flops=0, out=VMEM):
    return pl.pallas_call(
        kernel,
        out_shape=[jax.ShapeDtypeStruct(s, d) for s, d in outs],
        in_specs=[left.get(i, VMEM) for i in range(len(args))],
        out_specs=[out] * len(outs),
        scratch_shapes=list(scratch),
        compiler_params=pltpu.CompilerParams(vmem_limit_bytes=limit * 2**20),
        cost_estimate=pl.CostEstimate(flops=flops, bytes_accessed=0, transcendentals=0),
    )(*args)


def swap_near(count):
    return [i ^ 1 for i in range(count)]


def swap_far(count):
    return [None, *[i + 1 if i % 2 else i - 1 for i in range(1, count - 1)], None]


def exchange(block, axis, other, far):
    count, width = lax.axis_size(axis), lax.axis_size(other)
    partner = swap_far(count) if far else swap_near(count)
    aside = swap_near(width)
    moves = []
    for i in range(count):
        for j in range(width):
            to = (i, aside[j]) if partner[i] is None else (partner[i], j)
            if axis == "sx":
                moves.append((i * width + j, to[0] * width + to[1]))
            else:
                moves.append((j * count + i, to[1] * count + to[0]))
    return lax.ppermute(block, ("sx", "sy"), moves)


def pass_on(block, step):
    count_x, count_y, count = (lax.axis_size(a) for a in ("sx", "sy", "ch"))
    moves = []
    for x in range(count_x):
        for y in range(count_y):
            for c in range(count):
                to = (y ^ 1, c) if x in (0, count_x - 1) else (y, (c + step) % count)
                moves.append(((x * count_y + y) * count + c, (x * count_y + to[0]) * count + to[1]))
    return lax.ppermute(block, ("sx", "sy", "ch"), moves)


def odd(axis):
    return lax.rem(lax.axis_index(axis), 2) == 1


def at_end(axis):
    at = lax.axis_index(axis)
    return jnp.logical_or(at == 0, at == lax.axis_size(axis) - 1)


def to_rows(v_ref, rows_ref, near_ref, *far_ref):
    rows = jnp.swapaxes(v_ref[...], 0, 1)
    rows_ref[...] = rows
    is_odd = odd("sx")
    near_ref[...] = jnp.where(is_odd, rows[0], rows[-1])
    if far_ref:
        far_ref[0][...] = jnp.where(is_odd, rows[-1], rows[0])


def around(axis, near, far):
    is_odd = odd(axis)
    far = jnp.where(at_end(axis), jnp.zeros_like(far), far)
    return jnp.where(is_odd, near, far), jnp.where(is_odd, far, near)


def extended(rows_ref, near_ref, far_ref):
    before, after = around("sx", near_ref[...], far_ref[...])
    return [before, *[rows_ref[x] for x in range(rows_ref.shape[0])], after]


def pack(rows, start):
    cut = [r[:, start : start + CZ] for r in rows]
    part = rows[0].shape[0] // 4
    outer = jnp.concatenate([cut[0], cut[-1]], axis=1)
    folded = jnp.concatenate([outer[g * part : (g + 1) * part] for g in range(4)], axis=1)
    return jnp.concatenate([jnp.concatenate(cut[1:-1], axis=1), folded], axis=0)


def to_strips(rows_ref, near_ref, far_ref, _, near_strip_ref, far_strip_ref):
    rows = extended(rows_ref, near_ref, far_ref)
    low = pack(rows, 0)
    high = pack(rows, LANES - CZ)
    is_odd = odd("sy")
    near_strip_ref[...] = jnp.where(is_odd, low, high)
    far_strip_ref[...] = jnp.where(is_odd, high, low)


def inner_rows(cells_x):
    return list(range(1, cells_x - 1))


def shift_along_y(row, xs, x):
    lanes = row.shape[1]
    lane = lax.broadcasted_iota(jnp.int32, row.shape, 1)
    wide = row.astype(f32)
    xs[0, x] = jnp.where(lane < CZ, 0.0, pltpu.roll(wide, CZ, axis=1)).astype(bf16)
    xs[1, x] = jnp.where(lane >= lanes - CZ, 0.0, pltpu.roll(wide, lanes - CZ, axis=1)).astype(bf16)


def taps_of(weight_ref, a, b, step, channels, low=0, high=None):
    high = high or weight_ref.shape[3]
    outputs = pl.ds(low, high - low)
    if channels % LANES:
        taps = weight_ref[a, b, :, outputs, step * channels : (step + 1) * channels]
    else:
        count = lax.axis_size("ch")
        at = lax.rem(lax.axis_index("ch") + count - step, count)
        start = pl.multiple_of(at * channels, channels)
        taps = weight_ref[a, b, :, outputs, pl.ds(start, channels)]
    return taps.reshape(3 * (high - low), channels)


def tile_sum(weight_ref, step, rows, xs, tile, along_y, total=None):
    for b in along_y:
        for a in range(3):
            window = [rows[x + a] if b == 1 else xs[b // 2, x + a] for x in tile]
            rhs = jnp.concatenate(window, axis=1)
            taps = taps_of(weight_ref, a, b, step, rhs.shape[0])
            product = jnp.dot(taps, rhs, preferred_element_type=f32)
            total = product if total is None else total + product
    return total


def split(total):
    return [total[:, j : j + LANES] for j in range(0, total.shape[1], LANES)]


def strip_windows(strips_ref, channels):
    lanes, part = LANES, channels // 4
    size = channels + part
    near, far = strips_ref[0:size].astype(f32), strips_ref[size : 2 * size].astype(f32)
    lane = lax.broadcasted_iota(jnp.int32, (channels, lanes), 1)
    ends = []
    for strip in around("sy", near, far):
        main, folded = strip[:channels], strip[channels:]
        first, last = (
            jnp.concatenate(
                [pltpu.roll(folded, (to - at - g * 2 * CZ) % lanes, axis=1) for g in range(4)],
                axis=0,
            )
            for to, at in ((0, 0), (lanes - CZ, CZ))
        )
        windows = [
            jnp.where(lane < CZ, first, pltpu.roll(main, CZ, axis=1)),
            main,
            jnp.where(lane >= lanes - CZ, last, pltpu.roll(main, lanes - CZ, axis=1)),
        ]
        ends.append([w.astype(bf16) for w in windows])
    return ends


def strip_sums(weight_ref, step, ends, low=0, high=None):
    sums = []
    for b, windows in zip((0, 2), ends):
        total = None
        for a in range(3):
            taps = taps_of(weight_ref, a, b, step, windows[a].shape[0], low, high)
            product = jnp.dot(taps, windows[a], preferred_element_type=f32)
            total = product if total is None else total + product
        sums.append(total)
    return sums


def combine(row):
    outputs = row.shape[0] // 3
    cell = lax.rem(lax.broadcasted_iota(jnp.int32, (outputs, LANES), 1), CZ)
    under, mid, over = (row[c * outputs : (c + 1) * outputs] for c in range(3))
    under = jnp.where(cell == 0, 0.0, pltpu.roll(under, 1, axis=1))
    over = jnp.where(cell == CZ - 1, 0.0, pltpu.roll(over, LANES - 1, axis=1))
    return (under + over) + mid


def first_kernel(rows_ref, weight_ref, sum_ref, xs):
    cells_x = rows_ref.shape[0]
    rows = [None, *[rows_ref[x] for x in range(cells_x)]]
    tile = inner_rows(cells_x)[: sum_ref.shape[0]]
    for x in range(tile[0], tile[-1] + 3):
        shift_along_y(rows[x], xs, x)
    total = tile_sum(weight_ref, 0, rows, xs, tile, (1, 0, 2))
    for j, part in enumerate(split(total)):
        sum_ref[j] = part


def second_kernel(rows_ref, near_ref, far_ref, weight_ref, sum_ref, xs):
    rows = extended(rows_ref, near_ref, far_ref)
    last = rows_ref.shape[0] - 1
    done = rows_ref.shape[0] - sum_ref.shape[0]
    left = [*inner_rows(last + 1)[done:], 0, last]
    for x in range(last + 3):
        if any(x - a in left for a in range(3)):
            shift_along_y(rows[x], xs, x)
    for j in range(0, len(left), 2):
        total = tile_sum(weight_ref, 0, rows, xs, left[j : j + 2], (1, 0, 2))
        for i, part in enumerate(split(total)):
            sum_ref[j + i] = part


def join_kernel(near_ref, far_ref, far_row_ref, _, strips_ref):
    size = near_ref.shape[0]
    strips_ref[0:size] = near_ref[...]
    strips_ref[size : 2 * size] = far_ref[...]
    strips_ref[2 * size :] = far_row_ref[...]


def middle_kernel(others, *refs):
    strips_ref, weight_ref, one_ref, two_ref, bias_ref, *refs = refs
    rows_refs, near_refs = refs[:others], refs[others : 2 * others]
    sum_ref, ends_ref, xs = refs[2 * others :]
    cells_x, channels, _ = rows_refs[0].shape
    order = [*inner_rows(cells_x), 0, cells_x - 1]
    totals = [None] * (cells_x // 2)
    for i in range(others):
        near = near_refs[i][...]
        before, after = around("sx", near, jnp.zeros_like(near))
        rows = [before, *[rows_refs[i][x] for x in range(cells_x)], after]
        for x, row in enumerate(rows):
            shift_along_y(row, xs, x)
        for j in range(len(totals)):
            tile = order[2 * j : 2 * j + 2]
            totals[j] = tile_sum(weight_ref, i + 1, rows, xs, tile, (1, 0, 2), totals[j])
    kept = one_ref.shape[0]
    for j, part in enumerate(part for total in totals for part in split(total)):
        own = one_ref[j] if j < kept else two_ref[j - kept]
        sum_ref[order[j]] = combine(own + part) + bias_ref[...]
    for j, part in enumerate(strip_sums(weight_ref, 0, strip_windows(strips_ref, channels))):
        ends_ref[j] = part


def last_kernel(others, *refs):
    sum_ref, ends_ref, weight_ref, *passed_refs = refs[: 3 + others]
    out_ref, xs, stage, sems = refs[3 + others :]
    cells_x, outputs, lanes = sum_ref.shape
    channels = xs.shape[2]
    is_odd = odd("sx")
    far_tap = jnp.where(is_odd, 2, 0)
    ends, fars = [], []
    for i, ref in enumerate(passed_refs):
        ends.append(strip_windows(ref, channels))
        far = ref[pl.ds(ref.shape[0] - channels, channels)]
        far = jnp.where(at_end("sx"), jnp.zeros_like(far), far)
        shift_along_y(far, xs, i)
        fars.append(far)
    pieces = 2 if outputs % 32 == 0 else 1
    size = outputs // pieces
    lane = lax.broadcasted_iota(jnp.int32, (size, lanes), 1)
    copies = []
    for p in range(pieces):
        low, high = p * size, (p + 1) * size
        sums = [
            jnp.concatenate(
                [ends_ref[j, c * outputs + low : c * outputs + high] for c in range(3)], axis=0
            )
            for j in range(2)
        ]
        edge = None
        for i in range(others):
            parts = strip_sums(weight_ref, i + 1, ends[i], low, high)
            sums = [s + part for s, part in zip(sums, parts)]
            for b in range(3):
                taps = taps_of(weight_ref, far_tap, b, i + 1, channels, low, high)
                window = fars[i] if b == 1 else xs[b // 2, i]
                product = jnp.dot(taps, window, preferred_element_type=f32)
                edge = product if edge is None else edge + product
        first_end, last_end = (combine(s) for s in sums)
        edge = combine(edge)
        rows = []
        for x in range(cells_x):
            first = pltpu.roll(first_end, (-x * CZ) % lanes, axis=1)
            final = pltpu.roll(last_end, (lanes - CZ - x * CZ) % lanes, axis=1)
            row = sum_ref[x, low:high]
            if x == 0:
                row = row + jnp.where(is_odd, 0.0, edge)
            if x == cells_x - 1:
                row = row + jnp.where(is_odd, edge, 0.0)
            row = row + jnp.where(lane < CZ, first, jnp.where(lane >= lanes - CZ, final, 0.0))
            rows.append(row.astype(bf16))
        stage[low:high] = jnp.swapaxes(jnp.stack(rows), 0, 1)
        copies.append(
            pltpu.make_async_copy(stage.at[low:high], out_ref.at[low:high], sems.at[p])
        )
        copies[-1].start()
    for copy in copies:
        copy.wait()


def per_device(volume, weight, bias):
    channels, cells_x, lanes = volume.shape
    outputs = weight.shape[3]
    count = lax.axis_size("ch")
    others = count - 1
    strip = channels + channels // 4
    face, taps = (channels, lanes), (3 * outputs, lanes)
    half = cells_x // 2
    xs = pltpu.VMEM((2, cells_x + 2, *face), bf16)

    def along(step):
        return [(i, (i + step) % count) for i in range(count)]

    def rows_of(block, edges):
        return call(
            to_rows,
            [((cells_x, *face), bf16)] + [(face, bf16)] * edges,
            [block],
            flops=(edges - 1) * 10**10,
        )

    other_raw = [lax.ppermute(volume, "ch", along(step)) for step in range(1, count)]
    spread = jnp.broadcast_to(bias[:, None], (outputs, lanes))
    if channels % LANES:
        at = lax.axis_index("ch")
        blocks = [lax.rem(at + count - step, count) * channels for step in range(count)]
        weight = jnp.concatenate(
            [lax.dynamic_slice_in_dim(weight, i, channels, axis=4) for i in blocks], axis=4
        )
    rows, near, far = rows_of(volume, 2)
    near = exchange(near, "sx", "sy", False)
    far = exchange(far, "sx", "sy", True)
    (one,) = call(first_kernel, [((half, *taps), f32)], [rows, weight], [xs])
    low, high = call(to_strips, [((strip, lanes), bf16)] * 2, [rows, near, far, one], left={3: ANY})
    low = exchange(low, "sy", "sx", False)
    high = exchange(high, "sy", "sx", True)
    (two,) = call(
        second_kernel,
        [((cells_x - half, *taps), f32)],
        [rows, near, far, weight],
        [xs],
    )
    (strips,) = call(join_kernel, [((2 * strip + channels, lanes), bf16)], [low, high, far, two], left={3: ANY})
    other_strips = [lax.ppermute(strips, "ch", along(step)) for step in range(1, count)]
    other_rows, other_near = [], []
    for raw in other_raw:
        moved, edge = rows_of(raw, 1)
        other_rows.append(moved)
        other_near.append(exchange(edge, "sx", "sy", False))
    sums, ends = call(
        functools.partial(middle_kernel, others),
        [((cells_x, outputs, lanes), f32), ((2, *taps), f32)],
        [strips, weight, one, two, spread, *other_rows, *other_near],
        [xs],
    )
    return call(
        functools.partial(last_kernel, others),
        [((outputs, cells_x, lanes), bf16)],
        [sums, ends, weight, *other_strips],
        [
            pltpu.VMEM((2, others, *face), bf16),
            pltpu.VMEM((outputs, cells_x, lanes), bf16),
            pltpu.SemaphoreType.DMA((2,)),
        ],
        out=HBM,
    )[0]


def solution(mesh):
    return jax.shard_map(
        per_device,
        mesh=mesh,
        in_specs=(P("ch", "sx", "sy"), P(None, None, None, "ch", None), P("ch")),
        out_specs=P("ch", "sx", "sy"),
        check_vma=False,
    )
```

```python
import functools

import jax
import jax.numpy as jnp
from jax import lax
from jax.experimental import pallas as pl
from jax.experimental.pallas import tpu as pltpu
from jax.sharding import PartitionSpec as P

CZ = 16
LANES = 128
VMEM = pl.BlockSpec(memory_space=pltpu.VMEM)
HBM = pl.BlockSpec(memory_space=pltpu.HBM)
ANY = pl.BlockSpec(memory_space=pl.ANY)
bf16, f32 = jnp.bfloat16, jnp.float32


def call(kernel, outs, args, scratch=(), left={}, limit=24, flops=0, out=VMEM):
    return pl.pallas_call(
        kernel,
        out_shape=[jax.ShapeDtypeStruct(s, d) for s, d in outs],
        in_specs=[left.get(i, VMEM) for i in range(len(args))],
        out_specs=[out] * len(outs),
        scratch_shapes=list(scratch),
        compiler_params=pltpu.CompilerParams(vmem_limit_bytes=limit * 2**20),
        cost_estimate=pl.CostEstimate(flops=flops, bytes_accessed=0, transcendentals=0),
    )(*args)


def swap_near(count):
    return [i ^ 1 for i in range(count)]


def swap_far(count):
    return [None, *[i + 1 if i % 2 else i - 1 for i in range(1, count - 1)], None]


def exchange(block, axis, other, far):
    count, width = lax.axis_size(axis), lax.axis_size(other)
    partner = swap_far(count) if far else swap_near(count)
    aside = swap_near(width)
    moves = []
    for i in range(count):
        for j in range(width):
            to = (i, aside[j]) if partner[i] is None else (partner[i], j)
            if axis == "sx":
                moves.append((i * width + j, to[0] * width + to[1]))
            else:
                moves.append((j * count + i, to[1] * count + to[0]))
    return lax.ppermute(block, ("sx", "sy"), moves)


def pass_on(block, step):
    count_x, count_y, count = (lax.axis_size(a) for a in ("sx", "sy", "ch"))
    moves = []
    for x in range(count_x):
        for y in range(count_y):
            for c in range(count):
                to = (y ^ 1, c) if x in (0, count_x - 1) else (y, (c + step) % count)
                moves.append(((x * count_y + y) * count + c, (x * count_y + to[0]) * count + to[1]))
    return lax.ppermute(block, ("sx", "sy", "ch"), moves)


def odd(axis):
    return lax.rem(lax.axis_index(axis), 2) == 1


def at_end(axis):
    at = lax.axis_index(axis)
    return jnp.logical_or(at == 0, at == lax.axis_size(axis) - 1)


def ready_kernel(out_ref):
    out_ref[...] = jnp.zeros_like(out_ref)


def to_rows(edges, v_ref, *refs):
    rows_ref, near_ref, *far_ref = refs[len(refs) - 1 - edges :]
    rows = jnp.swapaxes(v_ref[...], 0, 1)
    rows_ref[...] = rows
    is_odd = odd("sx")
    near_ref[...] = jnp.where(is_odd, rows[0], rows[-1])
    if far_ref:
        far_ref[0][...] = jnp.where(is_odd, rows[-1], rows[0])


def around(axis, near, far):
    is_odd = odd(axis)
    far = jnp.where(at_end(axis), jnp.zeros_like(far), far)
    return jnp.where(is_odd, near, far), jnp.where(is_odd, far, near)


def extended(rows_ref, near_ref, far_ref):
    before, after = around("sx", near_ref[...], far_ref[...])
    return [before, *[rows_ref[x] for x in range(rows_ref.shape[0])], after]


def pack(rows, start):
    cut = [r[:, start : start + CZ] for r in rows]
    part = rows[0].shape[0] // 4
    outer = jnp.concatenate([cut[0], cut[-1]], axis=1)
    folded = jnp.concatenate([outer[g * part : (g + 1) * part] for g in range(4)], axis=1)
    return jnp.concatenate([jnp.concatenate(cut[1:-1], axis=1), folded], axis=0)


def to_strips(rows_ref, near_ref, far_ref, _, near_strip_ref, far_strip_ref):
    rows = extended(rows_ref, near_ref, far_ref)
    low = pack(rows, 0)
    high = pack(rows, LANES - CZ)
    is_odd = odd("sy")
    near_strip_ref[...] = jnp.where(is_odd, low, high)
    far_strip_ref[...] = jnp.where(is_odd, high, low)


def inner_rows(cells_x):
    return list(range(1, cells_x - 1))


def shift_along_y(row, xs, x):
    lanes = row.shape[1]
    lane = lax.broadcasted_iota(jnp.int32, row.shape, 1)
    wide = row.astype(f32)
    xs[0, x] = jnp.where(lane < CZ, 0.0, pltpu.roll(wide, CZ, axis=1)).astype(bf16)
    xs[1, x] = jnp.where(lane >= lanes - CZ, 0.0, pltpu.roll(wide, lanes - CZ, axis=1)).astype(bf16)


def taps_of(weight_ref, a, b, step, channels, low=0, high=None):
    high = high or weight_ref.shape[3]
    outputs = pl.ds(low, high - low)
    if channels % LANES:
        taps = weight_ref[a, b, :, outputs, step * channels : (step + 1) * channels]
    else:
        count = lax.axis_size("ch")
        at = lax.rem(lax.axis_index("ch") + count - step, count)
        start = pl.multiple_of(at * channels, channels)
        taps = weight_ref[a, b, :, outputs, pl.ds(start, channels)]
    return taps.reshape(3 * (high - low), channels)


def tile_sum(weight_ref, step, rows, xs, tile, along_y, total=None):
    for b in along_y:
        for a in range(3):
            window = [rows[x + a] if b == 1 else xs[b // 2, x + a] for x in tile]
            rhs = jnp.concatenate(window, axis=1)
            taps = taps_of(weight_ref, a, b, step, rhs.shape[0])
            product = jnp.dot(taps, rhs, preferred_element_type=f32)
            total = product if total is None else total + product
    return total


def split(total):
    return [total[:, j : j + LANES] for j in range(0, total.shape[1], LANES)]


def strip_windows(strips_ref, channels):
    lanes, part = LANES, channels // 4
    size = channels + part
    near, far = strips_ref[0:size].astype(f32), strips_ref[size : 2 * size].astype(f32)
    lane = lax.broadcasted_iota(jnp.int32, (channels, lanes), 1)
    ends = []
    for strip in around("sy", near, far):
        main, folded = strip[:channels], strip[channels:]
        first, last = (
            jnp.concatenate(
                [pltpu.roll(folded, (to - at - g * 2 * CZ) % lanes, axis=1) for g in range(4)],
                axis=0,
            )
            for to, at in ((0, 0), (lanes - CZ, CZ))
        )
        windows = [
            jnp.where(lane < CZ, first, pltpu.roll(main, CZ, axis=1)),
            main,
            jnp.where(lane >= lanes - CZ, last, pltpu.roll(main, lanes - CZ, axis=1)),
        ]
        ends.append([w.astype(bf16) for w in windows])
    return ends


def strip_sums(weight_ref, step, ends, low=0, high=None):
    sums = []
    for b, windows in zip((0, 2), ends):
        total = None
        for a in range(3):
            taps = taps_of(weight_ref, a, b, step, windows[a].shape[0], low, high)
            product = jnp.dot(taps, windows[a], preferred_element_type=f32)
            total = product if total is None else total + product
        sums.append(total)
    return sums


def combine(row):
    outputs = row.shape[0] // 3
    cell = lax.rem(lax.broadcasted_iota(jnp.int32, (outputs, LANES), 1), CZ)
    under, mid, over = (row[c * outputs : (c + 1) * outputs] for c in range(3))
    under = jnp.where(cell == 0, 0.0, pltpu.roll(under, 1, axis=1))
    over = jnp.where(cell == CZ - 1, 0.0, pltpu.roll(over, LANES - 1, axis=1))
    return (under + over) + mid


def first_kernel(rows_ref, weight_ref, sum_ref, xs):
    cells_x = rows_ref.shape[0]
    rows = [None, *[rows_ref[x] for x in range(cells_x)]]
    tile = inner_rows(cells_x)[: sum_ref.shape[0]]
    for x in range(tile[0], tile[-1] + 3):
        shift_along_y(rows[x], xs, x)
    total = tile_sum(weight_ref, 0, rows, xs, tile, (1, 0, 2))
    for j, part in enumerate(split(total)):
        sum_ref[j] = part


def second_kernel(rows_ref, near_ref, far_ref, weight_ref, sum_ref, xs):
    rows = extended(rows_ref, near_ref, far_ref)
    last = rows_ref.shape[0] - 1
    done = rows_ref.shape[0] - sum_ref.shape[0]
    left = [*inner_rows(last + 1)[done:], 0, last]
    for x in range(last + 3):
        if any(x - a in left for a in range(3)):
            shift_along_y(rows[x], xs, x)
    for j in range(0, len(left), 2):
        total = tile_sum(weight_ref, 0, rows, xs, left[j : j + 2], (1, 0, 2))
        for i, part in enumerate(split(total)):
            sum_ref[j + i] = part


def join_kernel(near_ref, far_ref, far_row_ref, _, strips_ref):
    size = near_ref.shape[0]
    strips_ref[0:size] = near_ref[...]
    strips_ref[size : 2 * size] = far_ref[...]
    strips_ref[2 * size :] = far_row_ref[...]


def ends_kernel(strips_ref, weight_ref, near_ref, ends_ref):
    windows = strip_windows(strips_ref, near_ref.shape[0])
    for j, part in enumerate(strip_sums(weight_ref, 0, windows)):
        ends_ref[j] = part


def inner_kernel(others, *refs):
    weight_ref, one_ref, two_ref, bias_ref, *refs = refs
    rows_refs, (sum_ref, xs) = refs[:others], refs[others:]
    cells_x = rows_refs[0].shape[0]
    order = inner_rows(cells_x)
    totals = [None] * (len(order) // 2)
    for i in range(others):
        rows = [None, *[rows_refs[i][x] for x in range(cells_x)]]
        for x in range(1, cells_x + 1):
            shift_along_y(rows[x], xs, x)
        for j in range(len(totals)):
            tile = order[2 * j : 2 * j + 2]
            totals[j] = tile_sum(weight_ref, i + 1, rows, xs, tile, (1, 0, 2), totals[j])
    kept = one_ref.shape[0]
    for j, part in enumerate(part for total in totals for part in split(total)):
        own = one_ref[j] if j < kept else two_ref[j - kept]
        sum_ref[j] = combine(own + part) + bias_ref[...]


def outer_kernel(others, *refs):
    weight_ref, two_ref, bias_ref, _, *refs = refs
    rows_refs, near_refs = refs[:others], refs[others : 2 * others]
    sum_ref, xs = refs[2 * others :]
    last = rows_refs[0].shape[0] - 1
    total = None
    for i in range(others):
        near = near_refs[i][...]
        before, after = around("sx", near, jnp.zeros_like(near))
        rows = [before, *[rows_refs[i][x] for x in range(last + 1)], after]
        for x in (0, 1, 2, last, last + 1, last + 2):
            shift_along_y(rows[x], xs, x)
        total = tile_sum(weight_ref, i + 1, rows, xs, (0, last), (1, 0, 2), total)
    done = two_ref.shape[0] - 2
    for j, part in enumerate(split(total)):
        sum_ref[j] = combine(two_ref[done + j] + part) + bias_ref[...]


def last_kernel(others, *refs):
    inner_ref, outer_ref, ends_ref, weight_ref, *passed_refs = refs[: 4 + others]
    out_ref, xs, stage, sems = refs[4 + others :]
    outputs, cells_x, lanes = stage.shape
    channels = xs.shape[2]
    is_odd = odd("sx")
    far_tap = jnp.where(is_odd, 2, 0)
    ends, fars = [], []
    for i, ref in enumerate(passed_refs):
        ends.append(strip_windows(ref, channels))
        far = ref[pl.ds(ref.shape[0] - channels, channels)]
        far = jnp.where(at_end("sx"), jnp.zeros_like(far), far)
        shift_along_y(far, xs, i)
        fars.append(far)
    pieces = 2 if outputs % 32 == 0 else 1
    size = outputs // pieces
    lane = lax.broadcasted_iota(jnp.int32, (size, lanes), 1)
    copies = []
    for p in range(pieces):
        low, high = p * size, (p + 1) * size
        sums = [
            jnp.concatenate(
                [ends_ref[j, c * outputs + low : c * outputs + high] for c in range(3)], axis=0
            )
            for j in range(2)
        ]
        edge = None
        for i in range(others):
            parts = strip_sums(weight_ref, i + 1, ends[i], low, high)
            sums = [s + part for s, part in zip(sums, parts)]
            for b in range(3):
                taps = taps_of(weight_ref, far_tap, b, i + 1, channels, low, high)
                window = fars[i] if b == 1 else xs[b // 2, i]
                product = jnp.dot(taps, window, preferred_element_type=f32)
                edge = product if edge is None else edge + product
        first_end, last_end = (combine(s) for s in sums)
        edge = combine(edge)
        rows = []
        for x in range(cells_x):
            first = pltpu.roll(first_end, (-x * CZ) % lanes, axis=1)
            final = pltpu.roll(last_end, (lanes - CZ - x * CZ) % lanes, axis=1)
            kept = outer_ref.at[x and 1] if x in (0, cells_x - 1) else inner_ref.at[x - 1]
            row = kept[low:high]
            if x == 0:
                row = row + jnp.where(is_odd, 0.0, edge)
            if x == cells_x - 1:
                row = row + jnp.where(is_odd, edge, 0.0)
            row = row + jnp.where(lane < CZ, first, jnp.where(lane >= lanes - CZ, final, 0.0))
            rows.append(row.astype(bf16))
        stage[low:high] = jnp.swapaxes(jnp.stack(rows), 0, 1)
        copies.append(
            pltpu.make_async_copy(stage.at[low:high], out_ref.at[low:high], sems.at[p])
        )
        copies[-1].start()
    for copy in copies:
        copy.wait()


def per_device(volume, weight, bias):
    channels, cells_x, lanes = volume.shape
    outputs = weight.shape[3]
    count = lax.axis_size("ch")
    others = count - 1
    strip = channels + channels // 4
    face, taps = (channels, lanes), (3 * outputs, lanes)
    half = cells_x // 2
    xs = pltpu.VMEM((2, cells_x + 2, *face), bf16)

    def along(step):
        return [(i, (i + step) % count) for i in range(count)]

    def rows_of(block, edges, *after):
        return call(
            functools.partial(to_rows, edges),
            [((cells_x, *face), bf16)] + [(face, bf16)] * edges,
            [block, *after],
            left={1: ANY},
            flops=(edges - 1) * 10**10,
        )

    other_raw = [lax.ppermute(volume, "ch", along(step)) for step in range(1, count)]
    spread = jnp.broadcast_to(bias[:, None], (outputs, lanes))
    if channels % LANES:
        at = lax.axis_index("ch")
        blocks = [lax.rem(at + count - step, count) * channels for step in range(count)]
        weight = jnp.concatenate(
            [lax.dynamic_slice_in_dim(weight, i, channels, axis=4) for i in blocks], axis=4
        )
    (ready,) = call(ready_kernel, [((8, lanes), f32)], [], flops=10**10)
    rows, near, far = rows_of(volume, 2, ready)
    near = exchange(near, "sx", "sy", False)
    far = exchange(far, "sx", "sy", True)
    (one,) = call(first_kernel, [((half, *taps), f32)], [rows, weight], [xs])
    low, high = call(to_strips, [((strip, lanes), bf16)] * 2, [rows, near, far, one], left={3: ANY})
    low = exchange(low, "sy", "sx", False)
    high = exchange(high, "sy", "sx", True)
    (two,) = call(
        second_kernel,
        [((cells_x - half, *taps), f32)],
        [rows, near, far, weight],
        [xs],
    )
    (strips,) = call(join_kernel, [((2 * strip + channels, lanes), bf16)], [low, high, far, two], left={3: ANY})
    other_strips = [lax.ppermute(strips, "ch", along(step)) for step in range(1, count)]
    (ends,) = call(ends_kernel, [((2, *taps), f32)], [strips, weight, near])
    other_rows, other_near = [], []
    for raw in other_raw:
        moved, edge = rows_of(raw, 1, ends)
        other_rows.append(moved)
        other_near.append(exchange(edge, "sx", "sy", False))
    (inner,) = call(
        functools.partial(inner_kernel, others),
        [((cells_x - 2, outputs, lanes), f32)],
        [weight, one, two, spread, *other_rows],
        [xs],
    )
    (outer,) = call(
        functools.partial(outer_kernel, others),
        [((2, outputs, lanes), f32)],
        [weight, two, spread, inner, *other_rows, *other_near],
        [xs],
        left={3: ANY},
    )
    return call(
        functools.partial(last_kernel, others),
        [((outputs, cells_x, lanes), bf16)],
        [inner, outer, ends, weight, *other_strips],
        [
            pltpu.VMEM((2, others, *face), bf16),
            pltpu.VMEM((outputs, cells_x, lanes), bf16),
            pltpu.SemaphoreType.DMA((2,)),
        ],
        out=HBM,
    )[0]


def solution(mesh):
    return jax.shard_map(
        per_device,
        mesh=mesh,
        in_specs=(P("ch", "sx", "sy"), P(None, None, None, "ch", None), P("ch")),
        out_specs=P("ch", "sx", "sy"),
        check_vma=False,
    )
```

```python
import functools

import jax
import jax.numpy as jnp
from jax import lax
from jax.experimental import pallas as pl
from jax.experimental.pallas import tpu as pltpu
from jax.sharding import PartitionSpec as P

CZ = 16
LANES = 128
VMEM = pl.BlockSpec(memory_space=pltpu.VMEM)
ANY = pl.BlockSpec(memory_space=pl.ANY)
bf16, f32 = jnp.bfloat16, jnp.float32


def call(kernel, outs, args, scratch=(), left={}, limit=24, flops=0):
    return pl.pallas_call(
        kernel,
        out_shape=[jax.ShapeDtypeStruct(s, d) for s, d in outs],
        in_specs=[left.get(i, VMEM) for i in range(len(args))],
        out_specs=[VMEM] * len(outs),
        scratch_shapes=list(scratch),
        compiler_params=pltpu.CompilerParams(vmem_limit_bytes=limit * 2**20),
        cost_estimate=pl.CostEstimate(flops=flops, bytes_accessed=0, transcendentals=0),
    )(*args)


def swap_near(count):
    return [i ^ 1 for i in range(count)]


def swap_far(count):
    return [None, *[i + 1 if i % 2 else i - 1 for i in range(1, count - 1)], None]


def exchange(block, axis, other, far):
    count, width = lax.axis_size(axis), lax.axis_size(other)
    partner = swap_far(count) if far else swap_near(count)
    aside = swap_near(width)
    moves = []
    for i in range(count):
        for j in range(width):
            to = (i, aside[j]) if partner[i] is None else (partner[i], j)
            if axis == "sx":
                moves.append((i * width + j, to[0] * width + to[1]))
            else:
                moves.append((j * count + i, to[1] * count + to[0]))
    return lax.ppermute(block, ("sx", "sy"), moves)


def pass_on(block, step):
    count_x, count_y, count = (lax.axis_size(a) for a in ("sx", "sy", "ch"))
    moves = []
    for x in range(count_x):
        for y in range(count_y):
            for c in range(count):
                to = (y ^ 1, c) if x in (0, count_x - 1) else (y, (c + step) % count)
                moves.append(((x * count_y + y) * count + c, (x * count_y + to[0]) * count + to[1]))
    return lax.ppermute(block, ("sx", "sy", "ch"), moves)


def odd(axis):
    return lax.rem(lax.axis_index(axis), 2) == 1


def at_end(axis):
    at = lax.axis_index(axis)
    return jnp.logical_or(at == 0, at == lax.axis_size(axis) - 1)


def ready_kernel(out_ref):
    out_ref[...] = jnp.zeros_like(out_ref)


def to_rows(edges, v_ref, *refs):
    rows_ref, near_ref, *far_ref = refs[len(refs) - 1 - edges :]
    rows = jnp.swapaxes(v_ref[...], 0, 1)
    rows_ref[...] = rows
    is_odd = odd("sx")
    near_ref[...] = jnp.where(is_odd, rows[0], rows[-1])
    if far_ref:
        far_ref[0][...] = jnp.where(is_odd, rows[-1], rows[0])


def around(axis, near, far):
    is_odd = odd(axis)
    far = jnp.where(at_end(axis), jnp.zeros_like(far), far)
    return jnp.where(is_odd, near, far), jnp.where(is_odd, far, near)


def extended(rows_ref, near_ref, far_ref):
    before, after = around("sx", near_ref[...], far_ref[...])
    return [before, *[rows_ref[x] for x in range(rows_ref.shape[0])], after]


def pack(rows, start):
    cut = [r[:, start : start + CZ] for r in rows]
    part = rows[0].shape[0] // 4
    outer = jnp.concatenate([cut[0], cut[-1]], axis=1)
    folded = jnp.concatenate([outer[g * part : (g + 1) * part] for g in range(4)], axis=1)
    return jnp.concatenate([jnp.concatenate(cut[1:-1], axis=1), folded], axis=0)


def to_strips(rows_ref, near_ref, far_ref, _, near_strip_ref, far_strip_ref):
    rows = extended(rows_ref, near_ref, far_ref)
    low = pack(rows, 0)
    high = pack(rows, LANES - CZ)
    is_odd = odd("sy")
    near_strip_ref[...] = jnp.where(is_odd, low, high)
    far_strip_ref[...] = jnp.where(is_odd, high, low)


def inner_rows(cells_x):
    return list(range(1, cells_x - 1))


def shift_along_y(row, xs, x):
    lanes = row.shape[1]
    lane = lax.broadcasted_iota(jnp.int32, row.shape, 1)
    wide = row.astype(f32)
    xs[0, x] = jnp.where(lane < CZ, 0.0, pltpu.roll(wide, CZ, axis=1)).astype(bf16)
    xs[1, x] = jnp.where(lane >= lanes - CZ, 0.0, pltpu.roll(wide, lanes - CZ, axis=1)).astype(bf16)


def taps_of(weight_ref, a, b, step, channels, low=0, high=None):
    high = high or weight_ref.shape[3]
    outputs = pl.ds(low, high - low)
    if channels % LANES:
        taps = weight_ref[a, b, :, outputs, step * channels : (step + 1) * channels]
    else:
        count = lax.axis_size("ch")
        at = lax.rem(lax.axis_index("ch") + count - step, count)
        start = pl.multiple_of(at * channels, channels)
        taps = weight_ref[a, b, :, outputs, pl.ds(start, channels)]
    return taps.reshape(3 * (high - low), channels)


def tile_sum(weight_ref, step, rows, xs, tile, along_y, total=None):
    for b in along_y:
        for a in range(3):
            window = [rows[x + a] if b == 1 else xs[b // 2, x + a] for x in tile]
            rhs = jnp.concatenate(window, axis=1)
            taps = taps_of(weight_ref, a, b, step, rhs.shape[0])
            product = jnp.dot(taps, rhs, preferred_element_type=f32)
            total = product if total is None else total + product
    return total


def split(total):
    return [total[:, j : j + LANES] for j in range(0, total.shape[1], LANES)]


def strip_windows(strips_ref, channels):
    lanes, part = LANES, channels // 4
    size = channels + part
    near, far = strips_ref[0:size].astype(f32), strips_ref[size : 2 * size].astype(f32)
    lane = lax.broadcasted_iota(jnp.int32, (channels, lanes), 1)
    ends = []
    for strip in around("sy", near, far):
        main, folded = strip[:channels], strip[channels:]
        first, last = (
            jnp.concatenate(
                [pltpu.roll(folded, (to - at - g * 2 * CZ) % lanes, axis=1) for g in range(4)],
                axis=0,
            )
            for to, at in ((0, 0), (lanes - CZ, CZ))
        )
        windows = [
            jnp.where(lane < CZ, first, pltpu.roll(main, CZ, axis=1)),
            main,
            jnp.where(lane >= lanes - CZ, last, pltpu.roll(main, lanes - CZ, axis=1)),
        ]
        ends.append([w.astype(bf16) for w in windows])
    return ends


def strip_sums(weight_ref, step, ends, low=0, high=None):
    sums = []
    for b, windows in zip((0, 2), ends):
        total = None
        for a in range(3):
            taps = taps_of(weight_ref, a, b, step, windows[a].shape[0], low, high)
            product = jnp.dot(taps, windows[a], preferred_element_type=f32)
            total = product if total is None else total + product
        sums.append(total)
    return sums


def combine(row):
    outputs = row.shape[0] // 3
    cell = lax.rem(lax.broadcasted_iota(jnp.int32, (outputs, LANES), 1), CZ)
    under, mid, over = (row[c * outputs : (c + 1) * outputs] for c in range(3))
    under = jnp.where(cell == 0, 0.0, pltpu.roll(under, 1, axis=1))
    over = jnp.where(cell == CZ - 1, 0.0, pltpu.roll(over, LANES - 1, axis=1))
    return (under + over) + mid


def first_kernel(rows_ref, weight_ref, sum_ref, xs):
    cells_x = rows_ref.shape[0]
    rows = [None, *[rows_ref[x] for x in range(cells_x)]]
    tile = inner_rows(cells_x)[: sum_ref.shape[0]]
    for x in range(tile[0], tile[-1] + 3):
        shift_along_y(rows[x], xs, x)
    total = tile_sum(weight_ref, 0, rows, xs, tile, (1, 0, 2))
    for j, part in enumerate(split(total)):
        sum_ref[j] = part


def second_kernel(rows_ref, near_ref, far_ref, weight_ref, sum_ref, xs):
    rows = extended(rows_ref, near_ref, far_ref)
    last = rows_ref.shape[0] - 1
    done = rows_ref.shape[0] - sum_ref.shape[0]
    left = [*inner_rows(last + 1)[done:], 0, last]
    for x in range(last + 3):
        if any(x - a in left for a in range(3)):
            shift_along_y(rows[x], xs, x)
    for j in range(0, len(left), 2):
        total = tile_sum(weight_ref, 0, rows, xs, left[j : j + 2], (1, 0, 2))
        for i, part in enumerate(split(total)):
            sum_ref[j + i] = part


def join_kernel(near_ref, far_ref, far_row_ref, _, strips_ref):
    size = near_ref.shape[0]
    strips_ref[0:size] = near_ref[...]
    strips_ref[size : 2 * size] = far_ref[...]
    strips_ref[2 * size :] = far_row_ref[...]


def ends_kernel(strips_ref, weight_ref, near_ref, ends_ref):
    windows = strip_windows(strips_ref, near_ref.shape[0])
    for j, part in enumerate(strip_sums(weight_ref, 0, windows)):
        ends_ref[j] = part


def inner_kernel(others, *refs):
    weight_ref, one_ref, two_ref, bias_ref, *refs = refs
    rows_refs, (sum_ref, xs) = refs[:others], refs[others:]
    cells_x = rows_refs[0].shape[0]
    order = inner_rows(cells_x)
    totals = [None] * (len(order) // 2)
    for i in range(others):
        rows = [None, *[rows_refs[i][x] for x in range(cells_x)]]
        for x in range(1, cells_x + 1):
            shift_along_y(rows[x], xs, x)
        for j in range(len(totals)):
            tile = order[2 * j : 2 * j + 2]
            totals[j] = tile_sum(weight_ref, i + 1, rows, xs, tile, (1, 0, 2), totals[j])
    kept = one_ref.shape[0]
    for j, part in enumerate(part for total in totals for part in split(total)):
        own = one_ref[j] if j < kept else two_ref[j - kept]
        sum_ref[j] = combine(own + part) + bias_ref[...]


def outer_kernel(others, *refs):
    weight_ref, two_ref, bias_ref, _, *refs = refs
    rows_refs, near_refs = refs[:others], refs[others : 2 * others]
    sum_ref, xs = refs[2 * others :]
    last = rows_refs[0].shape[0] - 1
    total = None
    for i in range(others):
        near = near_refs[i][...]
        before, after = around("sx", near, jnp.zeros_like(near))
        rows = [before, *[rows_refs[i][x] for x in range(last + 1)], after]
        for x in (0, 1, 2, last, last + 1, last + 2):
            shift_along_y(rows[x], xs, x)
        total = tile_sum(weight_ref, i + 1, rows, xs, (0, last), (1, 0, 2), total)
    done = two_ref.shape[0] - 2
    for j, part in enumerate(split(total)):
        sum_ref[j] = combine(two_ref[done + j] + part) + bias_ref[...]


def last_kernel(others, *refs):
    inner_ref, outer_ref, ends_ref, weight_ref, *passed_refs = refs[: 4 + others]
    out_ref, xs = refs[4 + others :]
    outputs, cells_x, lanes = out_ref.shape
    channels = xs.shape[2]
    is_odd = odd("sx")
    far_tap = jnp.where(is_odd, 2, 0)
    ends, fars = [], []
    for i, ref in enumerate(passed_refs):
        ends.append(strip_windows(ref, channels))
        far = ref[pl.ds(ref.shape[0] - channels, channels)]
        far = jnp.where(at_end("sx"), jnp.zeros_like(far), far)
        shift_along_y(far, xs, i)
        fars.append(far)
    pieces = 2 if outputs % 32 == 0 else 1
    size = outputs // pieces
    lane = lax.broadcasted_iota(jnp.int32, (size, lanes), 1)
    for p in range(pieces):
        low, high = p * size, (p + 1) * size
        sums = [
            jnp.concatenate(
                [ends_ref[j, c * outputs + low : c * outputs + high] for c in range(3)], axis=0
            )
            for j in range(2)
        ]
        edge = None
        for i in range(others):
            parts = strip_sums(weight_ref, i + 1, ends[i], low, high)
            sums = [s + part for s, part in zip(sums, parts)]
            for b in range(3):
                taps = taps_of(weight_ref, far_tap, b, i + 1, channels, low, high)
                window = fars[i] if b == 1 else xs[b // 2, i]
                product = jnp.dot(taps, window, preferred_element_type=f32)
                edge = product if edge is None else edge + product
        first_end, last_end = (combine(s) for s in sums)
        edge = combine(edge)
        rows = []
        for x in range(cells_x):
            first = pltpu.roll(first_end, (-x * CZ) % lanes, axis=1)
            final = pltpu.roll(last_end, (lanes - CZ - x * CZ) % lanes, axis=1)
            kept = outer_ref.at[x and 1] if x in (0, cells_x - 1) else inner_ref.at[x - 1]
            row = kept[low:high]
            if x == 0:
                row = row + jnp.where(is_odd, 0.0, edge)
            if x == cells_x - 1:
                row = row + jnp.where(is_odd, edge, 0.0)
            row = row + jnp.where(lane < CZ, first, jnp.where(lane >= lanes - CZ, final, 0.0))
            rows.append(row.astype(bf16))
        out_ref[low:high] = jnp.swapaxes(jnp.stack(rows), 0, 1)


def per_device(volume, weight, bias):
    channels, cells_x, lanes = volume.shape
    outputs = weight.shape[3]
    count = lax.axis_size("ch")
    others = count - 1
    strip = channels + channels // 4
    face, taps = (channels, lanes), (3 * outputs, lanes)
    half = cells_x // 2
    xs = pltpu.VMEM((2, cells_x + 2, *face), bf16)

    def along(step):
        return [(i, (i + step) % count) for i in range(count)]

    def rows_of(block, edges, *after):
        return call(
            functools.partial(to_rows, edges),
            [((cells_x, *face), bf16)] + [(face, bf16)] * edges,
            [block, *after],
            left={1: ANY},
            flops=(edges - 1) * 10**10,
        )

    other_raw = [lax.ppermute(volume, "ch", along(step)) for step in range(1, count)]
    spread = jnp.broadcast_to(bias[:, None], (outputs, lanes))
    if channels % LANES:
        at = lax.axis_index("ch")
        blocks = [lax.rem(at + count - step, count) * channels for step in range(count)]
        weight = jnp.concatenate(
            [lax.dynamic_slice_in_dim(weight, i, channels, axis=4) for i in blocks], axis=4
        )
    (ready,) = call(ready_kernel, [((8, lanes), f32)], [], flops=10**10)
    rows, near, far = rows_of(volume, 2, ready)
    near = exchange(near, "sx", "sy", False)
    far = exchange(far, "sx", "sy", True)
    (one,) = call(first_kernel, [((half, *taps), f32)], [rows, weight], [xs])
    low, high = call(to_strips, [((strip, lanes), bf16)] * 2, [rows, near, far, one], left={3: ANY})
    low = exchange(low, "sy", "sx", False)
    high = exchange(high, "sy", "sx", True)
    (two,) = call(
        second_kernel,
        [((cells_x - half, *taps), f32)],
        [rows, near, far, weight],
        [xs],
    )
    (strips,) = call(join_kernel, [((2 * strip + channels, lanes), bf16)], [low, high, far, two], left={3: ANY})
    other_strips = [lax.ppermute(strips, "ch", along(step)) for step in range(1, count)]
    (ends,) = call(ends_kernel, [((2, *taps), f32)], [strips, weight, near])
    other_rows, other_near = [], []
    for raw in other_raw:
        moved, edge = rows_of(raw, 1, ends)
        other_rows.append(moved)
        other_near.append(exchange(edge, "sx", "sy", False))
    (inner,) = call(
        functools.partial(inner_kernel, others),
        [((cells_x - 2, outputs, lanes), f32)],
        [weight, one, two, spread, *other_rows],
        [xs],
    )
    (outer,) = call(
        functools.partial(outer_kernel, others),
        [((2, outputs, lanes), f32)],
        [weight, two, spread, inner, *other_rows, *other_near],
        [xs],
        left={3: ANY},
    )
    return call(
        functools.partial(last_kernel, others),
        [((outputs, cells_x, lanes), bf16)],
        [inner, outer, ends, weight, *other_strips],
        [pltpu.VMEM((2, others, *face), bf16)],
    )[0]


def solution(mesh):
    return jax.shard_map(
        per_device,
        mesh=mesh,
        in_specs=(P("ch", "sx", "sy"), P(None, None, None, "ch", None), P("ch")),
        out_specs=P("ch", "sx", "sy"),
        check_vma=False,
    )
```

```python
import functools

import jax
import jax.numpy as jnp
from jax import lax
from jax.experimental import pallas as pl
from jax.experimental.pallas import tpu as pltpu
from jax.sharding import PartitionSpec as P

CZ = 16
LANES = 128
VMEM = pl.BlockSpec(memory_space=pltpu.VMEM)
ANY = pl.BlockSpec(memory_space=pl.ANY)
bf16, f32 = jnp.bfloat16, jnp.float32


def call(kernel, outs, args, scratch=(), left={}, limit=24, flops=0):
    return pl.pallas_call(
        kernel,
        out_shape=[jax.ShapeDtypeStruct(s, d) for s, d in outs],
        in_specs=[left.get(i, VMEM) for i in range(len(args))],
        out_specs=[VMEM] * len(outs),
        scratch_shapes=list(scratch),
        compiler_params=pltpu.CompilerParams(vmem_limit_bytes=limit * 2**20),
        cost_estimate=pl.CostEstimate(flops=flops, bytes_accessed=0, transcendentals=0),
    )(*args)


def swap_near(count):
    return [i ^ 1 for i in range(count)]


def swap_far(count):
    return [None, *[i + 1 if i % 2 else i - 1 for i in range(1, count - 1)], None]


def exchange(block, axis, other, far):
    count, width = lax.axis_size(axis), lax.axis_size(other)
    partner = swap_far(count) if far else swap_near(count)
    aside = swap_near(width)
    moves = []
    for i in range(count):
        for j in range(width):
            to = (i, aside[j]) if partner[i] is None else (partner[i], j)
            if axis == "sx":
                moves.append((i * width + j, to[0] * width + to[1]))
            else:
                moves.append((j * count + i, to[1] * count + to[0]))
    return lax.ppermute(block, ("sx", "sy"), moves)


def pass_on(block, step):
    count_x, count_y, count = (lax.axis_size(a) for a in ("sx", "sy", "ch"))
    moves = []
    for x in range(count_x):
        for y in range(count_y):
            for c in range(count):
                to = (y ^ 1, c) if x in (0, count_x - 1) else (y, (c + step) % count)
                moves.append(((x * count_y + y) * count + c, (x * count_y + to[0]) * count + to[1]))
    return lax.ppermute(block, ("sx", "sy", "ch"), moves)


def odd(axis):
    return lax.rem(lax.axis_index(axis), 2) == 1


def at_end(axis):
    at = lax.axis_index(axis)
    return jnp.logical_or(at == 0, at == lax.axis_size(axis) - 1)


def ready_kernel(out_ref):
    out_ref[...] = jnp.zeros_like(out_ref)


def to_rows(edges, v_ref, *refs):
    rows_ref, near_ref, *far_ref = refs[len(refs) - 1 - edges :]
    rows = jnp.swapaxes(v_ref[...], 0, 1)
    rows_ref[...] = rows
    is_odd = odd("sx")
    near_ref[...] = jnp.where(is_odd, rows[0], rows[-1])
    if far_ref:
        far_ref[0][...] = jnp.where(is_odd, rows[-1], rows[0])


def around(axis, near, far):
    is_odd = odd(axis)
    far = jnp.where(at_end(axis), jnp.zeros_like(far), far)
    return jnp.where(is_odd, near, far), jnp.where(is_odd, far, near)


def extended(rows_ref, near_ref, far_ref):
    before, after = around("sx", near_ref[...], far_ref[...])
    return [before, *[rows_ref[x] for x in range(rows_ref.shape[0])], after]


def pack(rows, start):
    cut = [r[:, start : start + CZ] for r in rows]
    part = rows[0].shape[0] // 4
    outer = jnp.concatenate([cut[0], cut[-1]], axis=1)
    folded = jnp.concatenate([outer[g * part : (g + 1) * part] for g in range(4)], axis=1)
    return jnp.concatenate([jnp.concatenate(cut[1:-1], axis=1), folded], axis=0)


def to_strips(rows_ref, near_ref, far_ref, _, near_strip_ref, far_strip_ref):
    rows = extended(rows_ref, near_ref, far_ref)
    low = pack(rows, 0)
    high = pack(rows, LANES - CZ)
    is_odd = odd("sy")
    near_strip_ref[...] = jnp.where(is_odd, low, high)
    far_strip_ref[...] = jnp.where(is_odd, high, low)


def inner_rows(cells_x):
    return list(range(1, cells_x - 1))


def shift_along_y(row, xs, x):
    lanes = row.shape[1]
    lane = lax.broadcasted_iota(jnp.int32, row.shape, 1)
    wide = row.astype(f32)
    xs[0, x] = jnp.where(lane < CZ, 0.0, pltpu.roll(wide, CZ, axis=1)).astype(bf16)
    xs[1, x] = jnp.where(lane >= lanes - CZ, 0.0, pltpu.roll(wide, lanes - CZ, axis=1)).astype(bf16)


def taps_of(weight_ref, a, b, step, channels, low=0, high=None):
    high = high or weight_ref.shape[3]
    outputs = pl.ds(low, high - low)
    if channels % LANES:
        taps = weight_ref[a, b, :, outputs, step * channels : (step + 1) * channels]
    else:
        count = lax.axis_size("ch")
        at = lax.rem(lax.axis_index("ch") + count - step, count)
        start = pl.multiple_of(at * channels, channels)
        taps = weight_ref[a, b, :, outputs, pl.ds(start, channels)]
    return taps.reshape(3 * (high - low), channels)


def tile_sum(weight_ref, step, rows, xs, tile, along_y, total=None):
    for b in along_y:
        for a in range(3):
            window = [rows[x + a] if b == 1 else xs[b // 2, x + a] for x in tile]
            rhs = jnp.concatenate(window, axis=1)
            taps = taps_of(weight_ref, a, b, step, rhs.shape[0])
            product = jnp.dot(taps, rhs, preferred_element_type=f32)
            total = product if total is None else total + product
    return total


def split(total):
    return [total[:, j : j + LANES] for j in range(0, total.shape[1], LANES)]


def strip_windows(strips_ref, channels):
    lanes, part = LANES, channels // 4
    size = channels + part
    near, far = strips_ref[0:size].astype(f32), strips_ref[size : 2 * size].astype(f32)
    lane = lax.broadcasted_iota(jnp.int32, (channels, lanes), 1)
    ends = []
    for strip in around("sy", near, far):
        main, folded = strip[:channels], strip[channels:]
        first, last = (
            jnp.concatenate(
                [pltpu.roll(folded, (to - at - g * 2 * CZ) % lanes, axis=1) for g in range(4)],
                axis=0,
            )
            for to, at in ((0, 0), (lanes - CZ, CZ))
        )
        windows = [
            jnp.where(lane < CZ, first, pltpu.roll(main, CZ, axis=1)),
            main,
            jnp.where(lane >= lanes - CZ, last, pltpu.roll(main, lanes - CZ, axis=1)),
        ]
        ends.append([w.astype(bf16) for w in windows])
    return ends


def strip_sums(weight_ref, step, ends, low=0, high=None):
    sums = []
    for b, windows in zip((0, 2), ends):
        total = None
        for a in range(3):
            taps = taps_of(weight_ref, a, b, step, windows[a].shape[0], low, high)
            product = jnp.dot(taps, windows[a], preferred_element_type=f32)
            total = product if total is None else total + product
        sums.append(total)
    return sums


def combine(row):
    outputs = row.shape[0] // 3
    cell = lax.rem(lax.broadcasted_iota(jnp.int32, (outputs, LANES), 1), CZ)
    under, mid, over = (row[c * outputs : (c + 1) * outputs] for c in range(3))
    under = jnp.where(cell == 0, 0.0, pltpu.roll(under, 1, axis=1))
    over = jnp.where(cell == CZ - 1, 0.0, pltpu.roll(over, LANES - 1, axis=1))
    return (under + over) + mid


def first_kernel(rows_ref, weight_ref, sum_ref, xs):
    cells_x = rows_ref.shape[0]
    rows = [None, *[rows_ref[x] for x in range(cells_x)]]
    tile = inner_rows(cells_x)[: sum_ref.shape[0]]
    for x in range(tile[0], tile[-1] + 3):
        shift_along_y(rows[x], xs, x)
    total = tile_sum(weight_ref, 0, rows, xs, tile, (1, 0, 2))
    for j, part in enumerate(split(total)):
        sum_ref[j] = part


def second_kernel(rows_ref, near_ref, far_ref, weight_ref, sum_ref, xs):
    rows = extended(rows_ref, near_ref, far_ref)
    last = rows_ref.shape[0] - 1
    done = rows_ref.shape[0] - sum_ref.shape[0]
    left = [*inner_rows(last + 1)[done:], 0, last]
    for x in range(last + 3):
        if any(x - a in left for a in range(3)):
            shift_along_y(rows[x], xs, x)
    for j in range(0, len(left), 2):
        total = tile_sum(weight_ref, 0, rows, xs, left[j : j + 2], (1, 0, 2))
        for i, part in enumerate(split(total)):
            sum_ref[j + i] = part


def join_kernel(near_ref, far_ref, far_row_ref, _, strips_ref):
    size = near_ref.shape[0]
    strips_ref[0:size] = near_ref[...]
    strips_ref[size : 2 * size] = far_ref[...]
    strips_ref[2 * size :] = far_row_ref[...]


def ends_kernel(strips_ref, weight_ref, near_ref, ends_ref):
    windows = strip_windows(strips_ref, near_ref.shape[0])
    for j, part in enumerate(strip_sums(weight_ref, 0, windows)):
        ends_ref[j] = combine(part)


def inner_kernel(others, *refs):
    weight_ref, one_ref, two_ref, bias_ref, *refs = refs
    rows_refs, (sum_ref, xs) = refs[:others], refs[others:]
    cells_x = rows_refs[0].shape[0]
    order = inner_rows(cells_x)
    totals = [None] * (len(order) // 2)
    for i in range(others):
        rows = [None, *[rows_refs[i][x] for x in range(cells_x)]]
        for x in range(1, cells_x + 1):
            shift_along_y(rows[x], xs, x)
        for j in range(len(totals)):
            tile = order[2 * j : 2 * j + 2]
            totals[j] = tile_sum(weight_ref, i + 1, rows, xs, tile, (1, 0, 2), totals[j])
    kept = one_ref.shape[0]
    for j, part in enumerate(part for total in totals for part in split(total)):
        own = one_ref[j] if j < kept else two_ref[j - kept]
        sum_ref[j] = combine(own + part) + bias_ref[...]


def outer_kernel(others, *refs):
    weight_ref, two_ref, bias_ref, _, *refs = refs
    rows_refs, near_refs = refs[:others], refs[others : 2 * others]
    sum_ref, xs = refs[2 * others :]
    last = rows_refs[0].shape[0] - 1
    total = None
    for i in range(others):
        near = near_refs[i][...]
        before, after = around("sx", near, jnp.zeros_like(near))
        rows = [before, *[rows_refs[i][x] for x in range(last + 1)], after]
        for x in (0, 1, 2, last, last + 1, last + 2):
            shift_along_y(rows[x], xs, x)
        total = tile_sum(weight_ref, i + 1, rows, xs, (0, last), (1, 0, 2), total)
    done = two_ref.shape[0] - 2
    for j, part in enumerate(split(total)):
        sum_ref[j] = combine(two_ref[done + j] + part) + bias_ref[...]


def last_kernel(others, *refs):
    inner_ref, outer_ref, ends_ref, weight_ref, *passed_refs = refs[: 4 + others]
    out_ref, xs = refs[4 + others :]
    outputs, cells_x, lanes = out_ref.shape
    channels = xs.shape[2]
    is_odd = odd("sx")
    far_tap = jnp.where(is_odd, 2, 0)
    ends, fars = [], []
    for i, ref in enumerate(passed_refs):
        ends.append(strip_windows(ref, channels))
        far = ref[pl.ds(ref.shape[0] - channels, channels)]
        far = jnp.where(at_end("sx"), jnp.zeros_like(far), far)
        shift_along_y(far, xs, i)
        fars.append(far)
    pieces = 2 if outputs % 32 == 0 else 1
    size = outputs // pieces
    lane = lax.broadcasted_iota(jnp.int32, (size, lanes), 1)
    for p in range(pieces):
        low, high = p * size, (p + 1) * size
        sums = edge = None
        for i in range(others):
            parts = strip_sums(weight_ref, i + 1, ends[i], low, high)
            sums = [s + part for s, part in zip(sums, parts)] if sums else parts
            for b in range(3):
                taps = taps_of(weight_ref, far_tap, b, i + 1, channels, low, high)
                window = fars[i] if b == 1 else xs[b // 2, i]
                product = jnp.dot(taps, window, preferred_element_type=f32)
                edge = product if edge is None else edge + product
        first_end, last_end = (combine(s) + ends_ref[j, low:high] for j, s in enumerate(sums))
        edge = combine(edge)
        rows = []
        for x in range(cells_x):
            first = pltpu.roll(first_end, (-x * CZ) % lanes, axis=1)
            final = pltpu.roll(last_end, (lanes - CZ - x * CZ) % lanes, axis=1)
            kept = outer_ref.at[x and 1] if x in (0, cells_x - 1) else inner_ref.at[x - 1]
            row = kept[low:high]
            if x == 0:
                row = row + jnp.where(is_odd, 0.0, edge)
            if x == cells_x - 1:
                row = row + jnp.where(is_odd, edge, 0.0)
            row = row + jnp.where(lane < CZ, first, jnp.where(lane >= lanes - CZ, final, 0.0))
            rows.append(row.astype(bf16))
        out_ref[low:high] = jnp.swapaxes(jnp.stack(rows), 0, 1)


def per_device(volume, weight, bias):
    channels, cells_x, lanes = volume.shape
    outputs = weight.shape[3]
    count = lax.axis_size("ch")
    others = count - 1
    strip = channels + channels // 4
    face, taps = (channels, lanes), (3 * outputs, lanes)
    half = cells_x // 2
    xs = pltpu.VMEM((2, cells_x + 2, *face), bf16)

    def along(step):
        return [(i, (i + step) % count) for i in range(count)]

    def rows_of(block, edges, *after):
        return call(
            functools.partial(to_rows, edges),
            [((cells_x, *face), bf16)] + [(face, bf16)] * edges,
            [block, *after],
            left={1: ANY},
            flops=(edges - 1) * 10**10,
        )

    other_raw = [lax.ppermute(volume, "ch", along(step)) for step in range(1, count)]
    spread = jnp.broadcast_to(bias[:, None], (outputs, lanes))
    if channels % LANES:
        at = lax.axis_index("ch")
        blocks = [lax.rem(at + count - step, count) * channels for step in range(count)]
        weight = jnp.concatenate(
            [lax.dynamic_slice_in_dim(weight, i, channels, axis=4) for i in blocks], axis=4
        )
    (ready,) = call(ready_kernel, [((8, lanes), f32)], [], flops=10**10)
    rows, near, far = rows_of(volume, 2, ready)
    near = exchange(near, "sx", "sy", False)
    far = exchange(far, "sx", "sy", True)
    (one,) = call(first_kernel, [((half, *taps), f32)], [rows, weight], [xs])
    low, high = call(to_strips, [((strip, lanes), bf16)] * 2, [rows, near, far, one], left={3: ANY})
    low = exchange(low, "sy", "sx", False)
    high = exchange(high, "sy", "sx", True)
    (two,) = call(
        second_kernel,
        [((cells_x - half, *taps), f32)],
        [rows, near, far, weight],
        [xs],
    )
    (strips,) = call(join_kernel, [((2 * strip + channels, lanes), bf16)], [low, high, far, two], left={3: ANY})
    other_strips = [lax.ppermute(strips, "ch", along(step)) for step in range(1, count)]
    (ends,) = call(ends_kernel, [((2, outputs, lanes), f32)], [strips, weight, near])
    other_rows, other_near = [], []
    for raw in other_raw:
        moved, edge = rows_of(raw, 1, ends)
        other_rows.append(moved)
        other_near.append(exchange(edge, "sx", "sy", False))
    (inner,) = call(
        functools.partial(inner_kernel, others),
        [((cells_x - 2, outputs, lanes), f32)],
        [weight, one, two, spread, *other_rows],
        [xs],
    )
    (outer,) = call(
        functools.partial(outer_kernel, others),
        [((2, outputs, lanes), f32)],
        [weight, two, spread, inner, *other_rows, *other_near],
        [xs],
        left={3: ANY},
    )
    return call(
        functools.partial(last_kernel, others),
        [((outputs, cells_x, lanes), bf16)],
        [inner, outer, ends, weight, *other_strips],
        [pltpu.VMEM((2, others, *face), bf16)],
    )[0]


def solution(mesh):
    return jax.shard_map(
        per_device,
        mesh=mesh,
        in_specs=(P("ch", "sx", "sy"), P(None, None, None, "ch", None), P("ch")),
        out_specs=P("ch", "sx", "sy"),
        check_vma=False,
    )
```

```python
import functools

import jax
import jax.numpy as jnp
from jax import lax
from jax.experimental import pallas as pl
from jax.experimental.pallas import tpu as pltpu
from jax.sharding import PartitionSpec as P

CZ = 16
LANES = 128
VMEM = pl.BlockSpec(memory_space=pltpu.VMEM)
ANY = pl.BlockSpec(memory_space=pl.ANY)
bf16, f32 = jnp.bfloat16, jnp.float32


def call(kernel, outs, args, scratch=(), left={}, limit=24, flops=0):
    return pl.pallas_call(
        kernel,
        out_shape=[jax.ShapeDtypeStruct(s, d) for s, d in outs],
        in_specs=[left.get(i, VMEM) for i in range(len(args))],
        out_specs=[VMEM] * len(outs),
        scratch_shapes=list(scratch),
        compiler_params=pltpu.CompilerParams(vmem_limit_bytes=limit * 2**20),
        cost_estimate=pl.CostEstimate(flops=flops, bytes_accessed=0, transcendentals=0),
    )(*args)


def swap_near(count):
    return [i ^ 1 for i in range(count)]


def swap_far(count):
    return [None, *[i + 1 if i % 2 else i - 1 for i in range(1, count - 1)], None]


def exchange(block, axis, other, far):
    count, width = lax.axis_size(axis), lax.axis_size(other)
    partner = swap_far(count) if far else swap_near(count)
    aside = swap_near(width)
    moves = []
    for i in range(count):
        for j in range(width):
            to = (i, aside[j]) if partner[i] is None else (partner[i], j)
            if axis == "sx":
                moves.append((i * width + j, to[0] * width + to[1]))
            else:
                moves.append((j * count + i, to[1] * count + to[0]))
    return lax.ppermute(block, ("sx", "sy"), moves)


def pass_on(block, step):
    count_x, count_y, count = (lax.axis_size(a) for a in ("sx", "sy", "ch"))
    moves = []
    for x in range(count_x):
        for y in range(count_y):
            for c in range(count):
                to = (y ^ 1, c) if x in (0, count_x - 1) else (y, (c + step) % count)
                moves.append(((x * count_y + y) * count + c, (x * count_y + to[0]) * count + to[1]))
    return lax.ppermute(block, ("sx", "sy", "ch"), moves)


def odd(axis):
    return lax.rem(lax.axis_index(axis), 2) == 1


def at_end(axis):
    at = lax.axis_index(axis)
    return jnp.logical_or(at == 0, at == lax.axis_size(axis) - 1)


def ready_kernel(out_ref):
    out_ref[...] = jnp.zeros_like(out_ref)


def to_rows(edges, v_ref, *refs):
    rows_ref, near_ref, *far_ref = refs[len(refs) - 1 - edges :]
    rows = jnp.swapaxes(v_ref[...], 0, 1)
    rows_ref[...] = rows
    is_odd = odd("sx")
    near_ref[...] = jnp.where(is_odd, rows[0], rows[-1])
    if far_ref:
        far_ref[0][...] = jnp.where(is_odd, rows[-1], rows[0])


def around(axis, near, far):
    is_odd = odd(axis)
    far = jnp.where(at_end(axis), jnp.zeros_like(far), far)
    return jnp.where(is_odd, near, far), jnp.where(is_odd, far, near)


def extended(rows_ref, near_ref, far_ref):
    before, after = around("sx", near_ref[...], far_ref[...])
    return [before, *[rows_ref[x] for x in range(rows_ref.shape[0])], after]


def pack(rows, start):
    cut = [r[:, start : start + CZ] for r in rows]
    part = rows[0].shape[0] // 4
    outer = jnp.concatenate([cut[0], cut[-1]], axis=1)
    folded = jnp.concatenate([outer[g * part : (g + 1) * part] for g in range(4)], axis=1)
    return jnp.concatenate([jnp.concatenate(cut[1:-1], axis=1), folded], axis=0)


def to_strips(rows_ref, near_ref, far_ref, _, near_strip_ref, far_strip_ref):
    rows = extended(rows_ref, near_ref, far_ref)
    low = pack(rows, 0)
    high = pack(rows, LANES - CZ)
    is_odd = odd("sy")
    near_strip_ref[...] = jnp.where(is_odd, low, high)
    far_strip_ref[...] = jnp.where(is_odd, high, low)


def inner_rows(cells_x):
    return list(range(1, cells_x - 1))


def shift_along_y(row, xs, x):
    lanes = row.shape[1]
    lane = lax.broadcasted_iota(jnp.int32, row.shape, 1)
    wide = row.astype(f32)
    xs[0, x] = jnp.where(lane < CZ, 0.0, pltpu.roll(wide, CZ, axis=1)).astype(bf16)
    xs[1, x] = jnp.where(lane >= lanes - CZ, 0.0, pltpu.roll(wide, lanes - CZ, axis=1)).astype(bf16)


def taps_of(weight_ref, a, b, step, channels, low=0, high=None):
    high = high or weight_ref.shape[3]
    outputs = pl.ds(low, high - low)
    if channels % LANES:
        taps = weight_ref[a, b, :, outputs, step * channels : (step + 1) * channels]
    else:
        count = lax.axis_size("ch")
        at = lax.rem(lax.axis_index("ch") + count - step, count)
        start = pl.multiple_of(at * channels, channels)
        taps = weight_ref[a, b, :, outputs, pl.ds(start, channels)]
    return taps.reshape(3 * (high - low), channels)


def tile_sum(weight_ref, step, rows, xs, tile, along_y, total=None):
    for b in along_y:
        for a in range(3):
            window = [rows[x + a] if b == 1 else xs[b // 2, x + a] for x in tile]
            rhs = jnp.concatenate(window, axis=1)
            taps = taps_of(weight_ref, a, b, step, rhs.shape[0])
            product = jnp.dot(taps, rhs, preferred_element_type=f32)
            total = product if total is None else total + product
    return total


def split(total):
    return [total[:, j : j + LANES] for j in range(0, total.shape[1], LANES)]


def strip_windows(strips_ref, channels):
    lanes, part = LANES, channels // 4
    size = channels + part
    near, far = strips_ref[0:size].astype(f32), strips_ref[size : 2 * size].astype(f32)
    lane = lax.broadcasted_iota(jnp.int32, (channels, lanes), 1)
    ends = []
    for strip in around("sy", near, far):
        main, folded = strip[:channels], strip[channels:]
        first, last = (
            jnp.concatenate(
                [pltpu.roll(folded, (to - at - g * 2 * CZ) % lanes, axis=1) for g in range(4)],
                axis=0,
            )
            for to, at in ((0, 0), (lanes - CZ, CZ))
        )
        windows = [
            jnp.where(lane < CZ, first, pltpu.roll(main, CZ, axis=1)),
            main,
            jnp.where(lane >= lanes - CZ, last, pltpu.roll(main, lanes - CZ, axis=1)),
        ]
        ends.append([w.astype(bf16) for w in windows])
    return ends


def strip_sums(weight_ref, step, ends, low=0, high=None):
    sums = []
    for b, windows in zip((0, 2), ends):
        total = None
        for a in range(3):
            taps = taps_of(weight_ref, a, b, step, windows[a].shape[0], low, high)
            product = jnp.dot(taps, windows[a], preferred_element_type=f32)
            total = product if total is None else total + product
        sums.append(total)
    return sums


def combine(row):
    outputs = row.shape[0] // 3
    cell = lax.rem(lax.broadcasted_iota(jnp.int32, (outputs, LANES), 1), CZ)
    under, mid, over = (row[c * outputs : (c + 1) * outputs] for c in range(3))
    under = jnp.where(cell == 0, 0.0, pltpu.roll(under, 1, axis=1))
    over = jnp.where(cell == CZ - 1, 0.0, pltpu.roll(over, LANES - 1, axis=1))
    return (under + over) + mid


def first_kernel(rows_ref, weight_ref, sum_ref, xs):
    cells_x = rows_ref.shape[0]
    rows = [None, *[rows_ref[x] for x in range(cells_x)]]
    tile = inner_rows(cells_x)[: sum_ref.shape[0]]
    for x in range(tile[0], tile[-1] + 3):
        shift_along_y(rows[x], xs, x)
    total = tile_sum(weight_ref, 0, rows, xs, tile, (1, 0, 2))
    for j, part in enumerate(split(total)):
        sum_ref[j] = part


def second_kernel(rows_ref, near_ref, far_ref, weight_ref, sum_ref, xs):
    rows = extended(rows_ref, near_ref, far_ref)
    last = rows_ref.shape[0] - 1
    done = rows_ref.shape[0] - sum_ref.shape[0]
    left = [*inner_rows(last + 1)[done:], 0, last]
    for x in range(last + 3):
        if any(x - a in left for a in range(3)):
            shift_along_y(rows[x], xs, x)
    for j in range(0, len(left), 2):
        total = tile_sum(weight_ref, 0, rows, xs, left[j : j + 2], (1, 0, 2))
        for i, part in enumerate(split(total)):
            sum_ref[j + i] = part


def join_kernel(far_ref, near_ref, far_row_ref, _, strips_ref):
    size = near_ref.shape[0]
    strips_ref[0:size] = near_ref[...]
    strips_ref[size : 2 * size] = far_ref[...]
    strips_ref[2 * size :] = far_row_ref[...]


def ends_kernel(strips_ref, weight_ref, near_ref, ends_ref):
    windows = strip_windows(strips_ref, near_ref.shape[0])
    for j, part in enumerate(strip_sums(weight_ref, 0, windows)):
        ends_ref[j] = combine(part)


def inner_kernel(others, *refs):
    weight_ref, one_ref, two_ref, bias_ref, *refs = refs
    rows_refs, (sum_ref, xs) = refs[:others], refs[others:]
    cells_x = rows_refs[0].shape[0]
    order = inner_rows(cells_x)
    totals = [None] * (len(order) // 2)
    for i in range(others):
        rows = [None, *[rows_refs[i][x] for x in range(cells_x)]]
        for x in range(1, cells_x + 1):
            shift_along_y(rows[x], xs, x)
        for j in range(len(totals)):
            tile = order[2 * j : 2 * j + 2]
            totals[j] = tile_sum(weight_ref, i + 1, rows, xs, tile, (1, 0, 2), totals[j])
    kept = one_ref.shape[0]
    for j, part in enumerate(part for total in totals for part in split(total)):
        own = one_ref[j] if j < kept else two_ref[j - kept]
        sum_ref[j] = combine(own + part) + bias_ref[...]


def outer_kernel(others, *refs):
    weight_ref, two_ref, bias_ref, _, *refs = refs
    rows_refs, near_refs = refs[:others], refs[others : 2 * others]
    sum_ref, xs = refs[2 * others :]
    last = rows_refs[0].shape[0] - 1
    total = None
    for i in range(others):
        near = near_refs[i][...]
        before, after = around("sx", near, jnp.zeros_like(near))
        rows = [before, *[rows_refs[i][x] for x in range(last + 1)], after]
        for x in (0, 1, 2, last, last + 1, last + 2):
            shift_along_y(rows[x], xs, x)
        total = tile_sum(weight_ref, i + 1, rows, xs, (0, last), (1, 0, 2), total)
    done = two_ref.shape[0] - 2
    for j, part in enumerate(split(total)):
        sum_ref[j] = combine(two_ref[done + j] + part) + bias_ref[...]


def last_kernel(others, *refs):
    inner_ref, outer_ref, ends_ref, weight_ref, *passed_refs = refs[: 4 + others]
    out_ref, xs = refs[4 + others :]
    outputs, cells_x, lanes = out_ref.shape
    channels = xs.shape[2]
    is_odd = odd("sx")
    far_tap = jnp.where(is_odd, 2, 0)
    ends, fars = [], []
    for i, ref in enumerate(passed_refs):
        ends.append(strip_windows(ref, channels))
        far = ref[pl.ds(ref.shape[0] - channels, channels)]
        far = jnp.where(at_end("sx"), jnp.zeros_like(far), far)
        shift_along_y(far, xs, i)
        fars.append(far)
    pieces = 2 if outputs % 32 == 0 else 1
    size = outputs // pieces
    lane = lax.broadcasted_iota(jnp.int32, (size, lanes), 1)
    for p in range(pieces):
        low, high = p * size, (p + 1) * size
        sums = edge = None
        for i in range(others):
            parts = strip_sums(weight_ref, i + 1, ends[i], low, high)
            sums = [s + part for s, part in zip(sums, parts)] if sums else parts
            for b in range(3):
                taps = taps_of(weight_ref, far_tap, b, i + 1, channels, low, high)
                window = fars[i] if b == 1 else xs[b // 2, i]
                product = jnp.dot(taps, window, preferred_element_type=f32)
                edge = product if edge is None else edge + product
        first_end, last_end = (combine(s) + ends_ref[j, low:high] for j, s in enumerate(sums))
        edge = combine(edge)
        rows = []
        for x in range(cells_x):
            first = pltpu.roll(first_end, (-x * CZ) % lanes, axis=1)
            final = pltpu.roll(last_end, (lanes - CZ - x * CZ) % lanes, axis=1)
            kept = outer_ref.at[x and 1] if x in (0, cells_x - 1) else inner_ref.at[x - 1]
            row = kept[low:high]
            if x == 0:
                row = row + jnp.where(is_odd, 0.0, edge)
            if x == cells_x - 1:
                row = row + jnp.where(is_odd, edge, 0.0)
            row = row + jnp.where(lane < CZ, first, jnp.where(lane >= lanes - CZ, final, 0.0))
            rows.append(row.astype(bf16))
        out_ref[low:high] = jnp.swapaxes(jnp.stack(rows), 0, 1)


def per_device(volume, weight, bias):
    channels, cells_x, lanes = volume.shape
    outputs = weight.shape[3]
    count = lax.axis_size("ch")
    others = count - 1
    strip = channels + channels // 4
    face, taps = (channels, lanes), (3 * outputs, lanes)
    half = cells_x // 2
    xs = pltpu.VMEM((2, cells_x + 2, *face), bf16)

    def along(step):
        return [(i, (i + step) % count) for i in range(count)]

    def rows_of(block, edges, *after):
        return call(
            functools.partial(to_rows, edges),
            [((cells_x, *face), bf16)] + [(face, bf16)] * edges,
            [block, *after],
            left={1: ANY},
            flops=(edges - 1) * 10**10,
        )

    other_raw = [lax.ppermute(volume, "ch", along(step)) for step in range(1, count)]
    spread = jnp.broadcast_to(bias[:, None], (outputs, lanes))
    if channels % LANES:
        at = lax.axis_index("ch")
        blocks = [lax.rem(at + count - step, count) * channels for step in range(count)]
        weight = jnp.concatenate(
            [lax.dynamic_slice_in_dim(weight, i, channels, axis=4) for i in blocks], axis=4
        )
    (ready,) = call(ready_kernel, [((8, lanes), f32)], [], flops=10**10)
    rows, near, far = rows_of(volume, 2, ready)
    near = exchange(near, "sx", "sy", False)
    far = exchange(far, "sx", "sy", True)
    (one,) = call(first_kernel, [((half, *taps), f32)], [rows, weight], [xs])
    low, high = call(to_strips, [((strip, lanes), bf16)] * 2, [rows, near, far, one], left={3: ANY})
    high = exchange(high, "sy", "sx", True)
    low = exchange(low, "sy", "sx", False)
    (two,) = call(
        second_kernel,
        [((cells_x - half, *taps), f32)],
        [rows, near, far, weight],
        [xs],
    )
    (strips,) = call(join_kernel, [((2 * strip + channels, lanes), bf16)], [high, low, far, two], left={3: ANY})
    other_strips = [lax.ppermute(strips, "ch", along(step)) for step in range(1, count)]
    (ends,) = call(ends_kernel, [((2, outputs, lanes), f32)], [strips, weight, near])
    other_rows, other_near = [], []
    for raw in other_raw:
        moved, edge = rows_of(raw, 1, ends)
        other_rows.append(moved)
        other_near.append(exchange(edge, "sx", "sy", False))
    (inner,) = call(
        functools.partial(inner_kernel, others),
        [((cells_x - 2, outputs, lanes), f32)],
        [weight, one, two, spread, *other_rows],
        [xs],
    )
    (outer,) = call(
        functools.partial(outer_kernel, others),
        [((2, outputs, lanes), f32)],
        [weight, two, spread, inner, *other_rows, *other_near],
        [xs],
        left={3: ANY},
    )
    return call(
        functools.partial(last_kernel, others),
        [((outputs, cells_x, lanes), bf16)],
        [inner, outer, ends, weight, *other_strips],
        [pltpu.VMEM((2, others, *face), bf16)],
    )[0]


def solution(mesh):
    return jax.shard_map(
        per_device,
        mesh=mesh,
        in_specs=(P("ch", "sx", "sy"), P(None, None, None, "ch", None), P("ch")),
        out_specs=P("ch", "sx", "sy"),
        check_vma=False,
    )
```
